512 devices in a mesh: ctx: 64 (over z, y), tp: 8 (over x, core).
Axes of the slice: x: 4, y: 8, z: 8, core: 2. Of those that a mesh axis runs over, the one named last changes fastest.
Arguments:
- enc: bfloat16 [1, 1408, 24576], P(None, 'tp', 'ctx'), may hold values from -6 to 6
- w_down: bfloat16 [5, 1408, 1536], P(None, 'tp', 'ctx'), may hold values from -0.15625 to 0.15625
- w_up: bfloat16 [5, 1536, 1408], P(None, 'tp', 'ctx'), may hold values from -0.15625 to 0.15625
- cot: bfloat16 [1, 1408, 24576], P(None, 'tp', 'ctx'), may hold values from -6 to 6
Outputs:
- merged: bfloat16 [1, 1408, 24576], P(None, 'tp', 'ctx')
- grad_enc: bfloat16 [1, 1408, 24576], P(None, 'tp', 'ctx')
The draws below stay inside these ranges and needn't reach their ends.
All inputs are finite; a program needn't handle non-finite values.
Results may differ from the reference program's by a relative error of at most 0.03.
Values may be sent and summed in bfloat16 or wider, within the bound.
A program may use at most 64 MiB of HBM per device.

```python
import jax
import jax.numpy as jnp
from jax import lax

FINE_CH = 1408
COARSE_CH = 1536
SEQS = 1
TAPS = 5
COARSE_LEN = 12288
FINE_LEN = 24576
N_TP = 8


def levels(rng, shape, cuts, smallest, largest):
    gain, own = 1.0, jax.random.fold_in(rng, 6)
    for position, shards_of in cuts:
        heights = jnp.exp(jax.random.uniform(jax.random.fold_in(own, position), (shards_of,), jnp.float32, smallest / len(cuts), largest / len(cuts)))
        gain = gain * jnp.repeat(heights, shape[position] // shards_of).reshape([-1 if axis == position else 1 for axis in range(len(shape))])
    return gain


def scatter_about(rng, dims, scale, most, cuts=(), kind=jnp.bfloat16):
    values = jax.random.normal(rng, dims, jnp.float32) * scale
    if len(cuts) > 0:
        values = levels(rng, dims, cuts, -0.22, 0.18) * values
    return jnp.clip(values, min=-most, max=most).astype(kind)


def setup_inputs(seed: int = 0) -> dict:
    key_list = jax.random.split(jax.random.key(seed), 5)
    enc = scatter_about(key_list[0], (SEQS, FINE_CH, FINE_LEN), 1.0, 6.0, ((1, 8), (2, 64)))
    w_down = scatter_about(key_list[1], (TAPS, FINE_CH, COARSE_CH), FINE_CH ** -0.5, 0.15625, ((1, 8), (2, 64)))
    w_up = scatter_about(key_list[2], (TAPS, COARSE_CH, FINE_CH), COARSE_CH ** -0.5, 0.15625, ((1, 8), (2, 64)))
    cot = scatter_about(key_list[3], (SEQS, FINE_CH, FINE_LEN), 1.0, 6.0, ((1, 8), (2, 64)))
    return {"enc": enc, "w_down": w_down, "w_up": w_up, "cot": cot}


root_half = 0.7071067811865476
norm_scale = 0.3989422804014327


def gelu_value(value):
    return 0.5 * value * (1.0 + jax.scipy.special.erf(value * root_half))


def gelu_slope(value):
    cumulative = 0.5 * (1.0 + jax.scipy.special.erf(value * root_half))
    return cumulative + value * jnp.exp(-0.5 * value * value) * norm_scale


def taps_sum(inputs, taps, rows):
    wide_in = inputs.astype(jnp.float32)
    wide_taps = taps.astype(jnp.float32)
    total = jnp.einsum("bcl,co->bol", wide_in[:, :, 0:rows], wide_taps[0])
    for offset in range(1, 5):
        total = total + jnp.einsum("bcl,co->bol", wide_in[:, :, offset:offset + rows], wide_taps[offset])
    return total


def group_conv(padded, weight, rows):
    width = weight.shape[1] // N_TP

    def add_group(total, index):
        inputs = lax.dynamic_slice_in_dim(padded, index * width, width, 1)
        taps = lax.dynamic_slice_in_dim(weight, index * width, width, 1)
        part = taps_sum(inputs, taps, rows)
        rounded = lax.optimization_barrier(part.astype(jnp.bfloat16)).astype(jnp.float32)
        return total + rounded, None

    start = jnp.zeros((padded.shape[0], weight.shape[2], rows), jnp.float32)
    total, unused = lax.scan(add_group, start, jnp.arange(N_TP, dtype=jnp.int32))
    return total


def back_conv(padded, weight, rows):
    wide_in = padded.astype(jnp.float32)
    wide_taps = weight.astype(jnp.float32)
    total = jnp.einsum("bol,co->bcl", wide_in[:, :, 4:4 + rows], wide_taps[0])
    for offset in range(1, 5):
        total = total + jnp.einsum("bol,co->bcl", wide_in[:, :, 4 - offset:4 - offset + rows], wide_taps[offset])
    return total


def pad_rows(values):
    return jnp.pad(values, ((0, 0), (0, 0), (2, 2)))


def reference(enc, w_down, w_up, cot):
    enc_wide = enc.astype(jnp.float32)
    pooled = (enc_wide.reshape(SEQS, FINE_CH, COARSE_LEN, 2).sum(axis=3) * 0.5).astype(jnp.bfloat16)
    pre_coarse = group_conv(pad_rows(pooled), w_down, COARSE_LEN)
    coarse = gelu_value(pre_coarse).astype(jnp.bfloat16)
    widened = jnp.repeat(coarse, 2, axis=2)
    pre_fine = group_conv(pad_rows(widened), w_up, FINE_LEN)
    merged = (enc_wide + gelu_value(pre_fine)).astype(jnp.bfloat16)
    grad_fine = (cot.astype(jnp.float32) * gelu_slope(pre_fine)).astype(jnp.bfloat16)
    grad_widened = back_conv(pad_rows(grad_fine), w_up, FINE_LEN)
    paired = grad_widened.reshape(SEQS, COARSE_CH, COARSE_LEN, 2).sum(axis=3)
    grad_coarse = (paired * gelu_slope(pre_coarse)).astype(jnp.bfloat16)
    grad_pooled = back_conv(pad_rows(grad_coarse), w_down, COARSE_LEN)
    grad_enc = (cot.astype(jnp.float32) + 0.5 * jnp.repeat(grad_pooled, 2, axis=2)).astype(jnp.bfloat16)
    return merged, grad_enc
```

```python
import jax
import jax.numpy as jnp
from jax import lax
from jax.experimental import pallas as pl
from jax.experimental.pallas import tpu as pltpu
from jax.sharding import PartitionSpec as P

MESH = pl.DeviceIdType.MESH
bf16 = jnp.bfloat16
f32 = jnp.float32
root_half = 0.7071067811865476
norm_scale = 0.3989422804014327

RING = 8
GROUPS = 8
FINE_C, COARSE_C = 176, 192
OUT1, OUT2 = 24, 22
ROWS = 24
L1, L2 = 896, 1024
POS, LANES, EDGE = 192, 256, 32
FINE = 384
WIDE = 128 + FINE + 128


def erf(value):
    return lax.erf(value)


def gelu_value(value):
    return 0.5 * value * (1.0 + erf(value * root_half))


def gelu_both(value):
    cumulative = 0.5 * (1.0 + erf(value * root_half))
    return value * cumulative, cumulative + value * jnp.exp(-0.5 * value * value) * norm_scale


def gelu_slope(value):
    return gelu_both(value)[1]


def dot(a, b):
    return jnp.dot(a, b, preferred_element_type=f32)


def dot_first(a, b):
    return lax.dot_general(a, b, (((0,), (0,)), ((), ())), preferred_element_type=f32)


def iota(shape, dim):
    return lax.broadcasted_iota(jnp.int32, shape, dim)


def flat(block):
    lanes = block.shape[-1]
    return block.astype(f32).reshape(RING * ROWS, lanes).astype(bf16)


def transposed(value, width):
    if width < LANES:
        value = jnp.concatenate([value, jnp.zeros((LANES, LANES - width), f32)], axis=1)
    return jnp.transpose(value)[:width]


def shift(value, amount, axis):
    size = value.shape[axis]
    return value if amount % size == 0 else pltpu.roll(value, amount % size, axis=axis)


def kernel(
    enc_ref, cot_ref, w1_ref, w2_ref, merged_ref, genc_ref,
    enc_wide, cot_wide, w1_all, w1_swap, w1_use, w2_all, w2_swap, w2_use,
    pooled_own, pooled_other, x1, p1_send, p1_recv, pre_c, c_own, c_other, x2,
    enc_rows, cot_rows, merged_rows, p2_send, p2_recv, g_send, g_recv, y1, y2, gc_out, gc_in,
    gc_send, gc_recv, y4, gp_out, gp_in,
    halo_s, halo_r, first_s, first_r, second_s, second_r, last_s, last_r, swap_s, swap_r,
    pair_s, pair_r, tp_s, tp_r,
):
    ctx, t = lax.axis_index("ctx"), lax.axis_index("tp")
    core = lax.rem(t, 2)
    mate = t + 1 - 2 * core
    z, y = lax.div(ctx, RING), lax.rem(ctx, RING)
    one = z + (y - z) * core
    two = y + (z - y) * core

    def ring(index, step):
        return lax.rem(index + RING + step, RING)

    def place(i, j):
        straight, crossed = i * RING + j, j * RING + i
        return straight + (crossed - straight) * core

    def remote(src, dst, send, recv, device):
        return pltpu.make_async_remote_copy(
            src_ref=src, dst_ref=dst, send_sem=send, recv_sem=recv, device_id=device, device_id_type=MESH
        )

    first_to = ((place(ring(one, 1), two), t), (place(ring(one, -1), two), t))
    second_to = ((place(one, ring(two, 1)), t), (place(one, ring(two, -1)), t))
    count = RING * RING
    ctx_next, ctx_prev = lax.rem(ctx + 1, count), lax.rem(ctx + count - 1, count)

    barrier = pltpu.get_barrier_semaphore()
    partners = [*first_to, *second_to, (ctx_next, t), (ctx_prev, t)]
    partners += [(ctx, lax.rem(t + d, GROUPS)) for d in range(1, GROUPS)]
    for device in partners:
        pl.semaphore_signal(barrier, inc=1, device_id=device, device_id_type=MESH)

    taps = ((w1_ref, w1_all, w1_swap), (w2_ref, w2_all, w2_swap))
    for w_ref, w_all, _ in taps:
        w_all[two, lax.div(one, 2), lax.rem(one, 2)] = w_ref[...]
    enc_wide[:, 128 : 128 + FINE] = enc_ref[...]
    cot_wide[:, 128 : 128 + FINE] = cot_ref[...]
    pl.semaphore_wait(barrier, len(partners))

    def halo(n, side):
        source, wide = ((enc_ref, enc_wide), (cot_ref, cot_wide))[n]
        if side == 0:
            src, dst, to = source.at[:, FINE - 128 : FINE], wide.at[:, 0:128], ctx_next
        else:
            src, dst, to = source.at[:, 0:128], wide.at[:, 128 + FINE : WIDE], ctx_prev
        return remote(src, dst, halo_s.at[n, side], halo_r.at[n, side], (to, t))

    def first(w, side, hop, arriving=False):
        step = hop if arriving else hop - 1
        index = ring(one, -step if side == 0 else step)
        block = taps[w][1].at[two, lax.div(index, 2), lax.rem(index, 2)]
        return remote(block, block, first_s.at[w, side, hop], first_r.at[w, side, hop], first_to[side])

    def second(w, side, hop, half, arriving=False):
        step = hop if arriving else hop - 1
        index = ring(two, -step if side == 0 else step)
        block = taps[w][1].at[index, pl.ds(2 * half, 2)]
        return remote(
            block, block, second_s.at[w, side, hop, half], second_r.at[w, side, hop, half], second_to[side]
        )

    def swap_zero(w, index):
        return remote(
            taps[w][1].at[index], taps[w][2].at[lax.div(index, 2)],
            swap_s.at[w, lax.div(index, 2)], swap_r.at[w, lax.div(index, 2)], (ctx, mate),
        )

    def swap_one(w, index):
        return remote(
            taps[w][1].at[index, :, 0], taps[w][2].at[:, lax.div(index, 2), lax.rem(index, 2)],
            swap_s.at[w, index], swap_r.at[w, index], (ctx, mate),
        )

    def swap(w, index):
        @pl.when(jnp.logical_and(core == 0, lax.rem(index, 2) == 1))
        def _():
            swap_zero(w, index).start()

        @pl.when(core == 1)
        def _():
            swap_one(w, index).start()

    def swap_done(w):
        @pl.when(core == 0)
        def _():
            for index in range(RING):
                swap_one(w, index).wait_recv()

        @pl.when(core == 1)
        def _():
            for index in range(1, RING, 2):
                swap_zero(w, index).wait_recv()

    def swap_sent(w):
        @pl.when(core == 0)
        def _():
            for index in range(1, RING, 2):
                swap_zero(w, index).wait_send()

        @pl.when(core == 1)
        def _():
            for index in range(RING):
                swap_one(w, index).wait_send()

    hops_first = {0: 4, 1: 3}

    def first_start(w, hop):
        for side in (0, 1):
            if hop <= hops_first[side]:
                first(w, side, hop).start()

    def first_step(w, hop):
        for side in (0, 1):
            if hop <= hops_first[side]:
                first(w, side, hop, True).wait_recv()
                if hop < hops_first[side]:
                    first(w, side, hop + 1).start()

    def second_start(w):
        for half in (0, 1):
            for side in (0, 1):
                second(w, side, 1, half).start()
        swap(w, two)

    def second_step(w, hop):
        if hop < 4:
            for half in (0, 1):
                for side in (0, 1):
                    second(w, side, hop, half, True).wait_recv()
                    if hop < 3 or half == side:
                        second(w, side, hop + 1, half).start()
            swap(w, ring(two, hop))
            swap(w, ring(two, -hop))
        else:
            for side in (0, 1):
                second(w, side, 4, side, True).wait_recv()
            swap(w, ring(two, 4))

    def pair(n, src, dst):
        return remote(src, dst, pair_s.at[n], pair_r.at[n], (ctx, mate))

    def to_group(n, d, src, dst):
        return remote(src, dst, tp_s.at[n, d], tp_r.at[n, d], (ctx, lax.rem(t + d, GROUPS)))

    def scatter(n, send, recv, d):
        return to_group(n, d, send.at[lax.rem(t + d, GROUPS)], recv.at[t])

    def gather(n, send, recv, d):
        return to_group(n, d, send.at[lax.rem(lax.rem(t + d, GROUPS), 2)], recv.at[t])

    order = (4, 3, 5, 2, 6, 1, 7)

    def pack_taps(w, q):
        w_all, w_swap, use, lanes = ((w1_all, w1_swap, w1_use, L1), (w2_all, w2_swap, w2_use, L2))[w]

        def put(block, other):
            if w == 0:
                use[q, :, other * L1 : (other + 1) * L1] = flat(block)
            else:
                use[q, :, other * 640 : (other + 1) * 640] = flat(block[..., 0:640])
                use[q, :, 1280 + other * 384 : 1280 + (other + 1) * 384] = flat(block[..., 640:1024])

        @pl.when(core == 0)
        def _():
            put(w_all[2 * q], 0)

        @pl.when(core == 1)
        def _():
            put(w_all[:, q, 1], 0)

        put(w_swap[q], 1)

    for n in (0, 1):
        for side in (0, 1):
            halo(n, side).start()
    first_start(0, 1)

    for hop in (1, 2, 3, 4):
        first_step(0, hop)
    second_start(0)
    first_start(1, 1)

    for n in (0, 1):
        for side in (0, 1):
            halo(n, side).wait_recv()
    lane = iota((WIDE, 2 * LANES), 1)
    row = iota((WIDE, 2 * LANES), 0)
    half_lane = lax.rem(lane, LANES)
    pick = jnp.where(row == 2 * half_lane + 64 + lax.div(lane, LANES), 1.0, 0.0).astype(bf16)
    where_to = iota((RING * ROWS, FINE_C), 1)
    spread = jnp.where(
        iota((RING * ROWS, FINE_C), 0) == lax.div(where_to, OUT2) * ROWS + lax.rem(where_to, OUT2), 1.0, 0.0
    ).astype(bf16)
    at = ctx * POS + iota((1, LANES), 1) - EDGE
    inside = jnp.logical_and(at >= 0, at < count * POS)
    enc_ed = dot(enc_wide[...], pick)
    pooled = jnp.where(inside, (enc_ed[:, 0:LANES] + enc_ed[:, LANES:]) * 0.5, 0.0)
    pooled_own[...] = pooled.astype(bf16)
    pair(0, pooled_own, pooled_other).start()
    first_step(1, 1)
    enc_rows[...] = dot(spread, enc_ed.astype(bf16)).reshape(RING, ROWS, 2 * LANES).astype(bf16)
    cot_ed = dot(cot_wide[...], pick).astype(bf16)
    cot_rows[...] = dot(spread, cot_ed).reshape(RING, ROWS, 2 * LANES).astype(bf16)
    first_step(1, 2)
    pair(0, pooled_own, pooled_other).wait_recv()
    for other, ref in enumerate((pooled_own, pooled_other)):
        value = ref[...].astype(f32)
        for k in range(5):
            start = other * L1 + k * FINE_C
            x1[start : start + FINE_C] = shift(value, 2 - k, 1).astype(bf16)
        x1[other * L1 + 880 : (other + 1) * L1] = jnp.zeros((16, LANES), bf16)
    first_step(1, 3)
    first_step(1, 4)
    second_step(0, 1)
    second_step(0, 2)
    second_step(0, 3)
    second_start(1)
    second_step(0, 4)
    swap_done(0)

    @pl.loop(0, 4)
    def _(q):
        pack_taps(0, q)
        part = dot(w1_use[q], x1[...])
        p1_send[:, q] = part.reshape(RING, ROWS, LANES).astype(bf16)

    for d in order:
        scatter(0, p1_send, p1_recv, d).start()
    p1_recv[t] = p1_send[t]
    second_step(1, 1)
    for d in order:
        scatter(0, p1_send, p1_recv, d).wait_recv()
    sides = [sum(p1_recv[2 * x + p].astype(f32) for x in range(4)) for p in (0, 1)]
    pre_c[...] = jnp.stack(sides, axis=1).reshape(COARSE_C, LANES)
    c_own[...] = jnp.where(inside, gelu_value(pre_c[...]), 0.0).astype(bf16)
    pair(1, c_own, c_other).start()
    second_step(1, 2)
    pair(1, c_own, c_other).wait_recv()
    for other, ref in enumerate((c_own, c_other)):
        value = ref[...]
        wide = value.astype(f32)
        before, after = shift(wide, 1, 1).astype(bf16), shift(wide, -1, 1).astype(bf16)
        for start, even, odd in (
            (other * 640, before, before),
            (other * 640 + 192, value, value),
            (other * 640 + 384, after, after),
            (1280 + other * 384, before, value),
            (1280 + other * 384 + 192, value, after),
        ):
            x2[start : start + COARSE_C, 0:LANES] = even
            x2[start : start + COARSE_C, LANES : 2 * LANES] = odd
        x2[other * 640 + 576 : (other + 1) * 640] = jnp.zeros((64, 2 * LANES), bf16)
    second_step(1, 3)
    second_step(1, 4)
    swap_done(1)

    @pl.loop(0, 4)
    def _(q):
        pack_taps(1, q)
        part = dot(w2_use[q], x2[...])
        p2_send[:, q] = part.reshape(RING, ROWS, 2 * LANES).astype(bf16)

    for d in order:
        scatter(1, p2_send, p2_recv, d).start()
    p2_recv[t] = p2_send[t]
    for d in order:
        scatter(1, p2_send, p2_recv, d).wait_recv()

    @pl.loop(0, 4)
    def _(q):
        for p in (0, 1):
            pre = sum(p2_recv[2 * x + p, q].astype(f32) for x in range(4))
            value, slope = gelu_both(pre)
            merged_rows[2 * q + p] = (enc_rows[2 * q + p].astype(f32) + value).astype(bf16)
            grad = (cot_rows[2 * q + p].astype(f32) * slope).astype(bf16).astype(f32)
            even = jnp.where(inside, grad[:, 0:LANES], 0.0)
            odd = jnp.where(inside, grad[:, LANES:], 0.0)
            g_send[p, q, :, 0:LANES] = (even + odd).astype(bf16)
            g_send[p, q, :, LANES : 2 * LANES] = (even + shift(odd, 1, 1)).astype(bf16)

    for d in order:
        gather(2, g_send, g_recv, d).start()
    g_recv[t] = g_send[core]

    back = iota((2 * LANES, FINE), 1)
    unpick = jnp.where(
        iota((2 * LANES, FINE), 0) == lax.rem(back, 2) * LANES + lax.div(back, 2) + EDGE, 1.0, 0.0
    ).astype(bf16)
    kept = dot_first(spread, flat(merged_rows[...])).astype(bf16)
    merged_ref[...] = dot(kept, unpick).astype(bf16)

    for d in order:
        gather(2, g_send, g_recv, d).wait_recv()
    y1[...] = jnp.zeros_like(y1)
    y2[...] = jnp.zeros_like(y2)

    @pl.loop(0, 4)
    def _(q):
        block = flat(g_recv[:, q])
        y1[...] += dot_first(block[:, 0:LANES], w2_use[q, :, 0:1280])
        y2[...] += dot_first(block[:, LANES:], w2_use[q, :, 1280:2048])

    def coarse_part(other):
        a, b = other * 640, other * 384
        total = shift(y1[:, a : a + 192] + y2[:, b : b + 192], -1, 0)
        total = total + y1[:, a + 192 : a + 384] + y2[:, b + 192 : b + 384]
        total = total + shift(y1[:, a + 384 : a + 576], 1, 0)
        return transposed(total, COARSE_C)

    gc_out[...] = coarse_part(1)
    pair(2, gc_out, gc_in).start()
    own = coarse_part(0)
    slope = gelu_slope(pre_c[...])
    pair(2, gc_out, gc_in).wait_recv()
    grad_c = jnp.where(inside, (own + gc_in[...]) * slope, 0.0).reshape(4, 2, ROWS, LANES).astype(bf16)
    gc_send[0] = grad_c[:, 0]
    gc_send[1] = grad_c[:, 1]
    for d in order:
        gather(3, gc_send, gc_recv, d).start()
    gc_recv[t] = gc_send[core]
    y4[...] = jnp.zeros_like(y4)
    for d in order:
        gather(3, gc_send, gc_recv, d).wait_recv()

    @pl.loop(0, 4)
    def _(q):
        y4[...] += dot_first(flat(gc_recv[:, q]), w1_use[q])

    def fine_part(other):
        total = None
        for k in range(5):
            start = other * L1 + k * FINE_C
            term = shift(y4[:, start : start + FINE_C], k - 2, 0)
            total = term if total is None else total + term
        return transposed(total, FINE_C)

    gp_out[...] = fine_part(1)
    pair(3, gp_out, gp_in).start()
    own = fine_part(0)
    coarse_row = iota((LANES, FINE), 0)
    widen = jnp.where(coarse_row == lax.div(iota((LANES, FINE), 1), 2) + EDGE, 1.0, 0.0).astype(bf16)
    pair(3, gp_out, gp_in).wait_recv()
    total = (own + gp_in[...]) * 0.5
    high = total.astype(bf16)
    low = (total - high.astype(f32)).astype(bf16)
    genc_ref[...] = (cot_ref[...].astype(f32) + dot(high, widen) + dot(low, widen)).astype(bf16)

    for n in (0, 1):
        for side in (0, 1):
            halo(n, side).wait_send()
    for w in (0, 1):
        for side in (0, 1):
            for hop in range(1, hops_first[side] + 1):
                first(w, side, hop).wait_send()
            for hop in (1, 2, 3):
                for half in (0, 1):
                    second(w, side, hop, half).wait_send()
            second(w, side, 4, side).wait_send()
        swap_sent(w)
    pair(0, pooled_own, pooled_other).wait_send()
    pair(1, c_own, c_other).wait_send()
    pair(2, gc_out, gc_in).wait_send()
    pair(3, gp_out, gp_in).wait_send()
    for d in order:
        scatter(0, p1_send, p1_recv, d).wait_send()
        scatter(1, p2_send, p2_recv, d).wait_send()
        gather(2, g_send, g_recv, d).wait_send()
        gather(3, gc_send, gc_recv, d).wait_send()


def shards(enc, w_down, w_up, cot):
    w1 = jnp.transpose(w_down, (2, 0, 1)).reshape(OUT1, 5 * FINE_C)
    w1 = jnp.pad(w1, ((0, 0), (0, L1 - 5 * FINE_C)))
    up = jnp.transpose(w_up, (2, 0, 1))
    even = up[:, 0::2].reshape(OUT2, 3 * COARSE_C)
    odd = up[:, 1::2].reshape(OUT2, 2 * COARSE_C)
    w2 = jnp.concatenate([jnp.pad(even, ((0, 0), (0, 64))), odd], axis=1)
    w2 = jnp.pad(w2, ((0, ROWS - OUT2), (0, 0)))
    dma = pltpu.SemaphoreType.DMA
    vmem = pltpu.VMEM
    merged, grad_enc = pl.pallas_call(
        kernel,
        out_shape=[jax.ShapeDtypeStruct((FINE_C, FINE), bf16)] * 2,
        in_specs=[pl.BlockSpec(memory_space=vmem)] * 4,
        out_specs=[pl.BlockSpec(memory_space=vmem)] * 2,
        scratch_shapes=[
            vmem((FINE_C, WIDE), bf16),
            vmem((FINE_C, WIDE), bf16),
            vmem((RING, 4, 2, ROWS, L1), bf16),
            vmem((4, 4, 2, ROWS, L1), bf16),
            vmem((4, RING * ROWS, 2 * L1), bf16),
            vmem((RING, 4, 2, ROWS, L2), bf16),
            vmem((4, 4, 2, ROWS, L2), bf16),
            vmem((4, RING * ROWS, 2 * L2), bf16),
            vmem((FINE_C, LANES), bf16),
            vmem((FINE_C, LANES), bf16),
            vmem((2 * L1, LANES), bf16),
            vmem((GROUPS, 4, ROWS, LANES), bf16),
            vmem((GROUPS, 4, ROWS, LANES), bf16),
            vmem((COARSE_C, LANES), f32),
            vmem((COARSE_C, LANES), bf16),
            vmem((COARSE_C, LANES), bf16),
            vmem((2 * L2, 2 * LANES), bf16),
            vmem((RING, ROWS, 2 * LANES), bf16),
            vmem((RING, ROWS, 2 * LANES), bf16),
            vmem((RING, ROWS, 2 * LANES), bf16),
            vmem((GROUPS, 4, ROWS, 2 * LANES), bf16),
            vmem((GROUPS, 4, ROWS, 2 * LANES), bf16),
            vmem((2, 4, ROWS, 2 * LANES), bf16),
            vmem((GROUPS, 4, ROWS, 2 * LANES), bf16),
            vmem((LANES, 1280), f32),
            vmem((LANES, 768), f32),
            vmem((COARSE_C, LANES), f32),
            vmem((COARSE_C, LANES), f32),
            vmem((2, 4, ROWS, LANES), bf16),
            vmem((GROUPS, 4, ROWS, LANES), bf16),
            vmem((LANES, 2 * L1), f32),
            vmem((FINE_C, LANES), f32),
            vmem((FINE_C, LANES), f32),
            dma((2, 2)),
            dma((2, 2)),
            dma((2, 2, 5)),
            dma((2, 2, 5)),
            dma((2, 2, 5, 2)),
            dma((2, 2, 5, 2)),
            dma((1,)),
            dma((1,)),
            dma((2, RING)),
            dma((2, RING)),
            dma((4,)),
            dma((4,)),
            dma((4, GROUPS)),
            dma((4, GROUPS)),
        ],
        compiler_params=pltpu.CompilerParams(
            collective_id=0, has_side_effects=True, vmem_limit_bytes=56 * 1024 * 1024
        ),
    )(enc[0], cot[0], w1, w2)
    return merged[None], grad_enc[None]


def solution(mesh):
    placed = P(None, "tp", "ctx")
    return jax.shard_map(
        shards,
        mesh=mesh,
        in_specs=(placed,) * 4,
        out_specs=(placed, placed),
        check_vma=False,
    )
```

```python
import functools

import jax
import jax.numpy as jnp
from jax import lax
from jax.experimental import pallas as pl
from jax.experimental.pallas import tpu as pltpu
from jax.sharding import PartitionSpec as P

MESH = pl.DeviceIdType.MESH
bf16 = jnp.bfloat16
f32 = jnp.float32
root_half = 0.7071067811865476
norm_scale = 0.3989422804014327

RING = 8
GROUPS = 8
FINE_C, COARSE_C = 176, 192
OUT1, OUT2 = 24, 22
ROWS = 24
L1, L2 = 896, 1024
POS, LANES, EDGE = 192, 256, 32
FINE = 384
WIDE = 128 + FINE + 128


def erf(value):
    return lax.erf(value)


def gelu_value(value):
    return 0.5 * value * (1.0 + erf(value * root_half))


def gelu_both(value):
    cumulative = 0.5 * (1.0 + erf(value * root_half))
    return value * cumulative, cumulative + value * jnp.exp(-0.5 * value * value) * norm_scale


def gelu_slope(value):
    return gelu_both(value)[1]


def dot(a, b):
    return jnp.dot(a, b, preferred_element_type=f32)


def dot_first(a, b):
    return lax.dot_general(a, b, (((0,), (0,)), ((), ())), preferred_element_type=f32)


def iota(shape, dim):
    return lax.broadcasted_iota(jnp.int32, shape, dim)


def flat(block):
    lanes = block.shape[-1]
    return block.reshape(RING * ROWS, lanes)


def transposed(value, width):
    if width < LANES:
        value = jnp.concatenate([value, jnp.zeros((LANES, LANES - width), f32)], axis=1)
    return jnp.transpose(value)[:width]


def shift(value, amount, axis):
    size = value.shape[axis]
    return value if amount % size == 0 else pltpu.roll(value, amount % size, axis=axis)


def kernel(
    enc_ref, cot_ref, w1_ref, w2_ref, merged_ref, genc_ref,
    enc_wide, cot_wide, w1_all, w1_swap, w2_all, w2_swap,
    pooled_own, pooled_other, x1, p1_send, p1_recv, pre_c, slope_c, c_own, c_other, x2,
    enc_rows, cot_rows, merged_rows, p2_send, p2_recv, g_send, g_recv, y1, y2, gc_out, gc_in,
    gc_send, gc_recv, y4, gp_out, gp_in,
    halo_s, halo_r, near_s, near_r, first_s, first_r, second_s, second_r, swap_s, swap_r,
    pair_s, pair_r, tp_s, tp_r,
):
    ctx, t = lax.axis_index("ctx"), lax.axis_index("tp")
    core = lax.rem(t, 2)
    mate = t + 1 - 2 * core
    z, y = lax.div(ctx, RING), lax.rem(ctx, RING)
    one = z + (y - z) * core
    two = y + (z - y) * core

    def ring(index, step):
        return lax.rem(index + RING + step, RING)

    def place(i, j):
        straight, crossed = i * RING + j, j * RING + i
        return straight + (crossed - straight) * core

    def remote(src, dst, send, recv, device):
        return pltpu.make_async_remote_copy(
            src_ref=src, dst_ref=dst, send_sem=send, recv_sem=recv, device_id=device, device_id_type=MESH
        )

    first_to = ((place(ring(one, 1), two), t), (place(ring(one, -1), two), t))
    second_to = ((place(one, ring(two, 1)), t), (place(one, ring(two, -1)), t))
    count = RING * RING
    ctx_next, ctx_prev = lax.rem(ctx + 1, count), lax.rem(ctx + count - 1, count)

    barrier = pltpu.get_barrier_semaphore()
    partners = [(place(ring(one, d), two), t) for d in range(1, RING)]
    partners += [*second_to, (ctx_next, t), (ctx_prev, t)]
    partners += [(ctx, lax.rem(t + d, GROUPS)) for d in range(1, GROUPS)]
    for device in partners:
        pl.semaphore_signal(barrier, inc=1, device_id=device, device_id_type=MESH)

    taps = ((w1_all, w1_swap), (w2_all, w2_swap))
    down = jnp.concatenate([w1_ref[k] for k in range(5)] + [jnp.zeros((16, OUT1), bf16)], axis=0).astype(f32)
    up = jnp.concatenate(
        [w2_ref[0], w2_ref[2], w2_ref[4], jnp.zeros((64, OUT2), bf16), w2_ref[1], w2_ref[3]], axis=0
    ).astype(f32)
    for w_all, tall in ((w1_all, down), (w2_all, up)):
        tall = jnp.concatenate([tall, jnp.zeros((tall.shape[0], 128 - tall.shape[1]), f32)], axis=1)
        w_all[two, lax.div(one, 2), lax.rem(one, 2)] = jnp.transpose(tall)[0:ROWS].astype(bf16)
    enc_wide[:, 128 : 128 + FINE] = enc_ref[...]
    cot_wide[:, 128 : 128 + FINE] = cot_ref[...]
    pl.semaphore_wait(barrier, len(partners))

    def halo(n, side):
        source, wide = ((enc_ref, enc_wide), (cot_ref, cot_wide))[n]
        if side == 0:
            src, dst, to = source.at[:, FINE - 128 : FINE], wide.at[:, 0:128], ctx_next
        else:
            src, dst, to = source.at[:, 0:128], wide.at[:, 128 + FINE : WIDE], ctx_prev
        return remote(src, dst, halo_s.at[n, side], halo_r.at[n, side], (to, t))

    def near(d):
        block = w1_all.at[two, lax.div(one, 2), lax.rem(one, 2)]
        return remote(block, block, near_s.at[d], near_r.at[d], (place(ring(one, d), two), t))

    def near_arrives(j):
        d = ring(one, -j)
        block = w1_all.at[two, lax.div(j, 2), lax.rem(j, 2)]
        remote(block, block, near_s.at[d], near_r.at[d], (place(ring(one, d), two), t)).wait_recv()

    def first(side, hop, arriving=False):
        step = hop if arriving else hop - 1
        index = ring(one, -step if side == 0 else step)
        block = w2_all.at[two, lax.div(index, 2), lax.rem(index, 2)]
        return remote(block, block, first_s.at[side, hop], first_r.at[side, hop], first_to[side])

    def piece(n):
        return lax.rem(lax.div(one, 2) + (0, 1, 3, 2)[n], 4)

    def second(w, side, hop, n, arriving=False):
        step = hop if arriving else hop - 1
        index = ring(two, -step if side == 0 else step)
        block = taps[w][0].at[index, piece(n)]
        return remote(block, block, second_s.at[w, side, hop, n], second_r.at[w, side, hop, n], second_to[side])

    def swap_zero(w, index):
        return remote(
            taps[w][0].at[index], taps[w][1].at[lax.div(index, 2)],
            swap_s.at[w, lax.div(index, 2)], swap_r.at[w, lax.div(index, 2)], (ctx, mate),
        )

    def swap_one(w, index):
        return remote(
            taps[w][0].at[index, :, 0], taps[w][1].at[:, lax.div(index, 2), lax.rem(index, 2)],
            swap_s.at[w, index], swap_r.at[w, index], (ctx, mate),
        )

    def swap(w, index):
        @pl.when(jnp.logical_and(core == 0, lax.rem(index, 2) == 1))
        def _():
            swap_zero(w, index).start()

        @pl.when(core == 1)
        def _():
            swap_one(w, index).start()

    def swap_done(w):
        @pl.when(core == 0)
        def _():
            for index in range(RING):
                swap_one(w, index).wait_recv()

        @pl.when(core == 1)
        def _():
            for index in range(1, RING, 2):
                swap_zero(w, index).wait_recv()

    def swap_sent(w):
        @pl.when(core == 0)
        def _():
            for index in range(1, RING, 2):
                swap_zero(w, index).wait_send()

        @pl.when(core == 1)
        def _():
            for index in range(RING):
                swap_one(w, index).wait_send()

    hops_first = {0: 4, 1: 3}

    def first_step(hop):
        for side in (0, 1):
            if hop <= hops_first[side]:
                if hop > 0:
                    first(side, hop, True).wait_recv()
                if hop < hops_first[side]:
                    first(side, hop + 1).start()

    def last_side(n):
        return 0 if n < 2 else 1

    def second_start(w, n):
        for side in (0, 1):
            second(w, side, 1, n).start()

    def second_step(w, hop):
        if hop < 4:
            for n in range(4):
                for side in (0, 1):
                    second(w, side, hop, n, True).wait_recv()
                    if hop < 3 or side == last_side(n):
                        second(w, side, hop + 1, n).start()
            swap(w, ring(two, hop))
            swap(w, ring(two, -hop))
        else:
            for n in range(4):
                second(w, last_side(n), 4, n, True).wait_recv()
            swap(w, ring(two, 4))

    def pair(n, src, dst):
        return remote(src, dst, pair_s.at[n], pair_r.at[n], (ctx, mate))

    def to_group(n, d, src, dst):
        return remote(src, dst, tp_s.at[n, d], tp_r.at[n, d], (ctx, lax.rem(t + d, GROUPS)))

    def scatter(n, c, send, recv, d):
        part = pl.ds(2 * c, 2)
        return to_group(n + c, d, send.at[lax.rem(t + d, GROUPS), part], recv.at[t, part])

    def gather(n, c, send, recv, d):
        part = pl.ds(2 * c, 2)
        return to_group(n + c, d, send.at[lax.rem(lax.rem(t + d, GROUPS), 2), part], recv.at[t, part])

    order = (4, 3, 5, 2, 6, 1, 7)

    def with_taps(w, q, use):
        w_all, w_swap = taps[w]

        @pl.when(core == 0)
        def _():
            use(flat(w_all[2 * q]), flat(w_swap[q]))

        @pl.when(core == 1)
        def _():
            use(flat(w_all[:, q, 1]), flat(w_swap[q]))

    for d in (1, 7, 2, 6, 3, 5, 4):
        near(d).start()
    near_arrives(one + 1 - 2 * lax.rem(one, 2))
    second_start(0, 0)
    for n in (1, 2, 3):
        near_arrives(2 * piece(n))
        near_arrives(2 * piece(n) + 1)
        second_start(0, n)
    swap(0, two)
    first_step(0)
    for n in (0, 1):
        for side in (0, 1):
            halo(n, side).start()

    lane = iota((WIDE, 2 * LANES), 1)
    row = iota((WIDE, 2 * LANES), 0)
    half_lane = lax.rem(lane, LANES)
    pick = jnp.where(row == 2 * half_lane + 64 + lax.div(lane, LANES), 1.0, 0.0).astype(bf16)
    where_to = iota((RING * ROWS, FINE_C), 1)
    spread = jnp.where(
        iota((RING * ROWS, FINE_C), 0) == lax.div(where_to, OUT2) * ROWS + lax.rem(where_to, OUT2), 1.0, 0.0
    ).astype(bf16)
    at = ctx * POS + iota((1, LANES), 1) - EDGE
    inside = jnp.logical_and(at >= 0, at < count * POS)
    second_step(0, 1)
    first_step(1)
    for n in (0, 1):
        for side in (0, 1):
            halo(n, side).wait_recv()
    enc_ed = dot(enc_wide[...], pick)
    pooled = jnp.where(inside, (enc_ed[:, 0:LANES] + enc_ed[:, LANES:]) * 0.5, 0.0)
    pooled_own[...] = pooled.astype(bf16)
    pair(0, pooled_own, pooled_other).start()
    second_step(0, 2)
    first_step(2)
    enc_rows[...] = dot(spread, enc_ed.astype(bf16)).reshape(RING, ROWS, 2 * LANES).astype(bf16)
    cot_ed = dot(cot_wide[...], pick).astype(bf16)
    cot_rows[...] = dot(spread, cot_ed).reshape(RING, ROWS, 2 * LANES).astype(bf16)
    pair(0, pooled_own, pooled_other).wait_recv()
    for other, ref in enumerate((pooled_own, pooled_other)):
        value = ref[...].astype(f32)
        for k in range(5):
            start = other * L1 + k * FINE_C
            x1[start : start + FINE_C] = shift(value, 2 - k, 1).astype(bf16)
        x1[other * L1 + 880 : (other + 1) * L1] = jnp.zeros((16, LANES), bf16)
    second_step(0, 3)
    first_step(3)
    first_step(4)
    for n in range(4):
        second_start(1, n)
    swap(1, two)
    second_step(0, 4)
    swap_done(0)

    for c in (0, 1):

        @pl.loop(2 * c, 2 * c + 2)
        def _(q):
            def use(mine, swapped):
                part = dot(mine, x1[0:L1]) + dot(swapped, x1[L1 : 2 * L1])
                p1_send[:, q] = part.reshape(RING, ROWS, LANES).astype(bf16)

            with_taps(0, q, use)

        for d in order:
            scatter(0, c, p1_send, p1_recv, d).start()

    p1_recv[t] = p1_send[t]
    second_step(1, 1)
    second_step(1, 2)
    for c in (0, 1):
        for d in order:
            scatter(0, c, p1_send, p1_recv, d).wait_recv()
    sides = [sum(p1_recv[2 * x + p].astype(f32) for x in range(4)) for p in (0, 1)]
    pre_c[...] = jnp.stack(sides, axis=1).reshape(COARSE_C, LANES)
    c_own[...] = jnp.where(inside, gelu_value(pre_c[...]), 0.0).astype(bf16)
    pair(1, c_own, c_other).start()
    slope_c[...] = gelu_slope(pre_c[...])
    pair(1, c_own, c_other).wait_recv()
    for other, ref in enumerate((c_own, c_other)):
        value = ref[...]
        wide = value.astype(f32)
        before, after = shift(wide, 1, 1).astype(bf16), shift(wide, -1, 1).astype(bf16)
        for start, even, odd in (
            (0, before, before),
            (192, value, value),
            (384, after, after),
            (640, before, value),
            (832, value, after),
        ):
            start += other * L2
            x2[start : start + COARSE_C, 0:LANES] = even
            x2[start : start + COARSE_C, LANES : 2 * LANES] = odd
        x2[other * L2 + 576 : other * L2 + 640] = jnp.zeros((64, 2 * LANES), bf16)
    second_step(1, 3)
    second_step(1, 4)
    swap_done(1)

    for c in (0, 1):

        @pl.loop(2 * c, 2 * c + 2)
        def _(q):
            def use(mine, swapped):
                part = dot(mine, x2[0:L2]) + dot(swapped, x2[L2 : 2 * L2])
                p2_send[:, q] = part.reshape(RING, ROWS, 2 * LANES).astype(bf16)

            with_taps(1, q, use)

        for d in order:
            scatter(2, c, p2_send, p2_recv, d).start()

    p2_recv[t] = p2_send[t]
    for c in (0, 1):
        for d in order:
            scatter(2, c, p2_send, p2_recv, d).wait_recv()

        @pl.loop(2 * c, 2 * c + 2)
        def _(q):
            for p in (0, 1):
                pre = sum(p2_recv[2 * x + p, q].astype(f32) for x in range(4))
                value, slope = gelu_both(pre)
                merged_rows[2 * q + p] = (enc_rows[2 * q + p].astype(f32) + value).astype(bf16)
                grad = (cot_rows[2 * q + p].astype(f32) * slope).astype(bf16).astype(f32)
                even = jnp.where(inside, grad[:, 0:LANES], 0.0)
                odd = jnp.where(inside, grad[:, LANES:], 0.0)
                g_send[p, q, :, 0:LANES] = (even + odd).astype(bf16)
                g_send[p, q, :, LANES : 2 * LANES] = (even + shift(odd, 1, 1)).astype(bf16)

        for d in order:
            gather(4, c, g_send, g_recv, d).start()
    g_recv[t] = g_send[core]

    back = iota((2 * LANES, FINE), 1)
    unpick = jnp.where(
        iota((2 * LANES, FINE), 0) == lax.rem(back, 2) * LANES + lax.div(back, 2) + EDGE, 1.0, 0.0
    ).astype(bf16)
    kept = dot_first(spread, flat(merged_rows[...])).astype(bf16)
    merged_ref[...] = dot(kept, unpick).astype(bf16)

    for c in (0, 1):
        for d in order:
            gather(4, c, g_send, g_recv, d).wait_recv()

        def add(mine, swapped, q):
            block = flat(g_recv[:, q])
            for other, use in enumerate((mine, swapped)):
                sums = dot_first(block[:, 0:LANES], use[:, 0:640])
                pairs = dot_first(block[:, LANES:], use[:, 640:1024])
                if q == 0:
                    y1[other], y2[other] = sums, pairs
                else:
                    y1[other] += sums
                    y2[other] += pairs

        for q in (2 * c, 2 * c + 1):
            with_taps(1, q, functools.partial(add, q=q))

    def coarse_part(other):
        total = shift(y1[other, :, 0:192] + y2[other, :, 0:192], -1, 0)
        total = total + y1[other, :, 192:384] + y2[other, :, 192:384]
        total = total + shift(y1[other, :, 384:576], 1, 0)
        return transposed(total, COARSE_C)

    gc_out[...] = coarse_part(1)
    pair(2, gc_out, gc_in).start()
    own = coarse_part(0)
    pair(2, gc_out, gc_in).wait_recv()
    grad_c = jnp.where(inside, (own + gc_in[...]) * slope_c[...], 0.0).reshape(4, 2, ROWS, LANES).astype(bf16)
    gc_send[0] = grad_c[:, 0]
    gc_send[1] = grad_c[:, 1]
    for c in (0, 1):
        for d in order:
            gather(6, c, gc_send, gc_recv, d).start()
    gc_recv[t] = gc_send[core]
    coarse_row = iota((LANES, FINE), 0)
    widen = jnp.where(coarse_row == lax.div(iota((LANES, FINE), 1), 2) + EDGE, 1.0, 0.0).astype(bf16)
    for c in (0, 1):
        for d in order:
            gather(6, c, gc_send, gc_recv, d).wait_recv()

        def add(mine, swapped, q):
            block = flat(gc_recv[:, q])
            for other, use in enumerate((mine, swapped)):
                if q == 0:
                    y4[other] = dot_first(block, use)
                else:
                    y4[other] += dot_first(block, use)

        for q in (2 * c, 2 * c + 1):
            with_taps(0, q, functools.partial(add, q=q))

    def fine_part(other):
        total = None
        for k in range(5):
            term = shift(y4[other, :, k * FINE_C : (k + 1) * FINE_C], k - 2, 0)
            total = term if total is None else total + term
        return transposed(total, FINE_C)

    gp_out[...] = fine_part(1)
    pair(3, gp_out, gp_in).start()
    own = fine_part(0)
    pair(3, gp_out, gp_in).wait_recv()
    total = (own + gp_in[...]) * 0.5
    high = total.astype(bf16)
    low = (total - high.astype(f32)).astype(bf16)
    genc_ref[...] = (cot_ref[...].astype(f32) + dot(high, widen) + dot(low, widen)).astype(bf16)

    for n in (0, 1):
        for side in (0, 1):
            halo(n, side).wait_send()
    for d in range(1, RING):
        near(d).wait_send()
    for side in (0, 1):
        for hop in range(1, hops_first[side] + 1):
            first(side, hop).wait_send()
    for w in (0, 1):
        for side in (0, 1):
            for n in range(4):
                for hop in (1, 2, 3, 4):
                    if hop < 4 or side == last_side(n):
                        second(w, side, hop, n).wait_send()
        swap_sent(w)
    pair(0, pooled_own, pooled_other).wait_send()
    pair(1, c_own, c_other).wait_send()
    pair(2, gc_out, gc_in).wait_send()
    pair(3, gp_out, gp_in).wait_send()
    for c in (0, 1):
        for d in order:
            scatter(0, c, p1_send, p1_recv, d).wait_send()
            scatter(2, c, p2_send, p2_recv, d).wait_send()
            gather(4, c, g_send, g_recv, d).wait_send()
            gather(6, c, gc_send, gc_recv, d).wait_send()


def shards(enc, w_down, w_up, cot):
    dma = pltpu.SemaphoreType.DMA
    vmem = pltpu.VMEM
    merged, grad_enc = pl.pallas_call(
        kernel,
        out_shape=[jax.ShapeDtypeStruct((FINE_C, FINE), bf16)] * 2,
        in_specs=[pl.BlockSpec(memory_space=vmem)] * 4,
        out_specs=[pl.BlockSpec(memory_space=vmem)] * 2,
        scratch_shapes=[
            vmem((FINE_C, WIDE), bf16),
            vmem((FINE_C, WIDE), bf16),
            vmem((RING, 4, 2, ROWS, L1), bf16),
            vmem((4, 4, 2, ROWS, L1), bf16),
            vmem((RING, 4, 2, ROWS, L2), bf16),
            vmem((4, 4, 2, ROWS, L2), bf16),
            vmem((FINE_C, LANES), bf16),
            vmem((FINE_C, LANES), bf16),
            vmem((2 * L1, LANES), bf16),
            vmem((GROUPS, 4, ROWS, LANES), bf16),
            vmem((GROUPS, 4, ROWS, LANES), bf16),
            vmem((COARSE_C, LANES), f32),
            vmem((COARSE_C, LANES), f32),
            vmem((COARSE_C, LANES), bf16),
            vmem((COARSE_C, LANES), bf16),
            vmem((2 * L2, 2 * LANES), bf16),
            vmem((RING, ROWS, 2 * LANES), bf16),
            vmem((RING, ROWS, 2 * LANES), bf16),
            vmem((RING, ROWS, 2 * LANES), bf16),
            vmem((GROUPS, 4, ROWS, 2 * LANES), bf16),
            vmem((GROUPS, 4, ROWS, 2 * LANES), bf16),
            vmem((2, 4, ROWS, 2 * LANES), bf16),
            vmem((GROUPS, 4, ROWS, 2 * LANES), bf16),
            vmem((2, LANES, 640), f32),
            vmem((2, LANES, 384), f32),
            vmem((COARSE_C, LANES), f32),
            vmem((COARSE_C, LANES), f32),
            vmem((2, 4, ROWS, LANES), bf16),
            vmem((GROUPS, 4, ROWS, LANES), bf16),
            vmem((2, LANES, L1), f32),
            vmem((FINE_C, LANES), f32),
            vmem((FINE_C, LANES), f32),
            dma((2, 2)),
            dma((2, 2)),
            dma((RING,)),
            dma((RING,)),
            dma((2, 5)),
            dma((2, 5)),
            dma((2, 2, 5, 4)),
            dma((2, 2, 5, 4)),
            dma((2, RING)),
            dma((2, RING)),
            dma((4,)),
            dma((4,)),
            dma((8, GROUPS)),
            dma((8, GROUPS)),
        ],
        compiler_params=pltpu.CompilerParams(
            collective_id=0, has_side_effects=True, vmem_limit_bytes=56 * 1024 * 1024
        ),
    )(enc[0], cot[0], w_down, w_up)
    return merged[None], grad_enc[None]


def solution(mesh):
    placed = P(None, "tp", "ctx")
    return jax.shard_map(
        shards,
        mesh=mesh,
        in_specs=(placed,) * 4,
        out_specs=(placed, placed),
        check_vma=False,
    )
```

```python
import jax
import jax.numpy as jnp
from jax import lax
from jax.experimental import pallas as pl
from jax.experimental.pallas import tpu as pltpu
from jax.sharding import PartitionSpec as P

MESH = pl.DeviceIdType.MESH
bf16 = jnp.bfloat16
f32 = jnp.float32
root_half = 0.7071067811865476
norm_scale = 0.3989422804014327

RING = 8
GROUPS = 8
FINE_C, COARSE_C = 176, 192
OUT1, OUT2 = 24, 22
ROWS = 24
L1, L2 = 896, 1024
POS, LANES, EDGE = 192, 256, 32
FINE = 384
WIDE = 128 + FINE + 128
VMEM_LIMIT = 36 << 20


def erf(value):
    return lax.erf(value)


def gelu_value(value):
    return 0.5 * value * (1.0 + erf(value * root_half))


def gelu_both(value):
    cumulative = 0.5 * (1.0 + erf(value * root_half))
    return value * cumulative, cumulative + value * jnp.exp(-0.5 * value * value) * norm_scale


def gelu_slope(value):
    return gelu_both(value)[1]


def dot(a, b):
    return jnp.dot(a, b, preferred_element_type=f32)


def dot_first(a, b):
    return lax.dot_general(a, b, (((0,), (0,)), ((), ())), preferred_element_type=f32)


def iota(shape, dim):
    return lax.broadcasted_iota(jnp.int32, shape, dim)


def flat(block):
    lanes = block.shape[-1]
    return block.reshape(RING * ROWS, lanes)


def transposed(value, width):
    if width < LANES:
        value = jnp.concatenate([value, jnp.zeros((LANES, LANES - width), f32)], axis=1)
    return jnp.transpose(value)[:width]


def shift(value, amount, axis):
    size = value.shape[axis]
    return value if amount % size == 0 else pltpu.roll(value, amount % size, axis=axis)


def kernel(
    enc_ref, cot_ref, w1_ref, w2_ref, merged_ref, genc_ref,
    edge_out, edge_in, enc_wide, cot_wide, w1_all, w1_swap, w2_all, w2_swap,
    pooled_own, pooled_other, x1, p1_send, p1_recv, pre_c, slope_c, c_own, c_other, x2,
    enc_rows, cot_rows, merged_rows, p2_send, p2_recv, g_send, g_recv, y1, y2, gc_out, gc_in,
    gc_send, gc_recv, y4, gp_out, gp_in,
    halo_s, halo_r, near_s, near_r, first_s, first_r, second_s, second_r, swap_s, swap_r,
    pair_s, pair_r, tp_s, tp_r,
):
    ctx, t = lax.axis_index("ctx"), lax.axis_index("tp")
    core = lax.rem(t, 2)
    mate = t + 1 - 2 * core
    z, y = lax.div(ctx, RING), lax.rem(ctx, RING)
    one = z + (y - z) * core
    two = y + (z - y) * core

    def ring(index, step):
        return lax.rem(index + RING + step, RING)

    def place(i, j):
        straight, crossed = i * RING + j, j * RING + i
        return straight + (crossed - straight) * core

    def remote(src, dst, send, recv, device):
        return pltpu.make_async_remote_copy(
            src_ref=src, dst_ref=dst, send_sem=send, recv_sem=recv, device_id=device, device_id_type=MESH
        )

    second_to = ((place(one, ring(two, 1)), t), (place(one, ring(two, -1)), t))
    count = RING * RING
    ctx_next, ctx_prev = lax.rem(ctx + 1, count), lax.rem(ctx + count - 1, count)

    barrier = pltpu.get_barrier_semaphore()
    partners = [(place(ring(one, d), two), t) for d in range(1, RING)]
    partners += [*second_to, (ctx_next, t), (ctx_prev, t)]
    partners += [(ctx, lax.rem(t + d, GROUPS)) for d in range(1, GROUPS)]
    for device in partners:
        pl.semaphore_signal(barrier, inc=1, device_id=device, device_id_type=MESH)

    taps = ((w1_all, w1_swap), (w2_all, w2_swap))
    down = [w1_ref[k].astype(f32) for k in range(5)]
    up = [w2_ref[k].astype(f32) for k in range(5)]
    down = jnp.concatenate([*down, jnp.zeros((OUT1, 16), f32)], axis=1)
    up = jnp.concatenate([up[0], up[2], up[4], jnp.zeros((OUT2, 64), f32), up[1], up[3]], axis=1)
    up = jnp.concatenate([up, jnp.zeros((ROWS - OUT2, L2), f32)], axis=0)
    for w_all, block in ((w1_all, down), (w2_all, up)):
        w_all[two, lax.div(one, 2), lax.rem(one, 2)] = block.astype(bf16)
    enc_wide[:, 128 : 128 + FINE] = enc_ref[...]
    cot_wide[:, 128 : 128 + FINE] = cot_ref[...]
    low = iota((FINE_C, 128), 1) < 64
    last, first_tile = slice(FINE - 128, FINE), slice(0, 128)
    enc_last, cot_last = enc_ref[:, last].astype(f32), shift(cot_ref[:, last].astype(f32), 64, 1)
    enc_first, cot_first = enc_ref[:, first_tile].astype(f32), shift(cot_ref[:, first_tile].astype(f32), 64, 1)
    edge_out[0] = jnp.where(low, cot_last, enc_last).astype(bf16)
    edge_out[1] = jnp.where(low, enc_first, cot_first).astype(bf16)
    pl.semaphore_wait(barrier, len(partners))

    def halo(side):
        to = ctx_next if side == 0 else ctx_prev
        return remote(edge_out.at[side], edge_in.at[side], halo_s.at[side], halo_r.at[side], (to, t))

    def near(d):
        block = w1_all.at[two, lax.div(one, 2), lax.rem(one, 2)]
        return remote(block, block, near_s.at[d], near_r.at[d], (place(ring(one, d), two), t))

    def near_arrives(j):
        d = ring(one, -j)
        block = w1_all.at[two, lax.div(j, 2), lax.rem(j, 2)]
        remote(block, block, near_s.at[d], near_r.at[d], (place(ring(one, d), two), t)).wait_recv()

    routes = ((0, 1), (0, -1), (0, 2), (0, -2), (-2, 1), (-2, 2), (2, -1))

    def first(m, arriving=False):
        origin, step = routes[m]
        index = ring(one, origin - step if arriving else origin)
        block = w2_all.at[two, lax.div(index, 2), lax.rem(index, 2)]
        return remote(block, block, first_s.at[m], first_r.at[m], (place(ring(one, step), two), t))

    def piece(n):
        return lax.rem(lax.div(one, 2) + (0, 1, 3, 2)[n], 4)

    def second(w, side, hop, n, arriving=False):
        step = hop if arriving else hop - 1
        index = ring(two, -step if side == 0 else step)
        block = taps[w][0].at[index, piece(n)]
        return remote(block, block, second_s.at[w, side, hop, n], second_r.at[w, side, hop, n], second_to[side])

    def swap_zero(w, index):
        return remote(
            taps[w][0].at[index], taps[w][1].at[lax.div(index, 2)],
            swap_s.at[w, lax.div(index, 2)], swap_r.at[w, lax.div(index, 2)], (ctx, mate),
        )

    def swap_one(w, index):
        return remote(
            taps[w][0].at[index, :, 0], taps[w][1].at[:, lax.div(index, 2), lax.rem(index, 2)],
            swap_s.at[w, index], swap_r.at[w, index], (ctx, mate),
        )

    def swap(w, index):
        @pl.when(jnp.logical_and(core == 0, lax.rem(index, 2) == 1))
        def _():
            swap_zero(w, index).start()

        @pl.when(core == 1)
        def _():
            swap_one(w, index).start()

    def swap_done(w):
        @pl.when(core == 0)
        def _():
            for index in range(RING):
                swap_one(w, index).wait_recv()

        @pl.when(core == 1)
        def _():
            for index in range(1, RING, 2):
                swap_zero(w, index).wait_recv()

    def swap_sent(w):
        @pl.when(core == 0)
        def _():
            for index in range(1, RING, 2):
                swap_zero(w, index).wait_send()

        @pl.when(core == 1)
        def _():
            for index in range(RING):
                swap_one(w, index).wait_send()

    def last_side(n):
        return 0 if n < 2 else 1

    def second_start(w, n):
        for side in (0, 1):
            second(w, side, 1, n).start()

    def second_part(w, hop, n):
        for side in (0, 1):
            second(w, side, hop, n, True).wait_recv()
            if hop < 3 or side == last_side(n):
                second(w, side, hop + 1, n).start()

    def second_swap(w, hop):
        swap(w, ring(two, hop))
        swap(w, ring(two, -hop))

    def second_step(w, hop):
        if hop < 4:
            for n in range(4):
                second_part(w, hop, n)
            second_swap(w, hop)
        else:
            for n in range(4):
                second(w, last_side(n), 4, n, True).wait_recv()
            swap(w, ring(two, 4))

    def pair(n, src, dst):
        return remote(src, dst, pair_s.at[n], pair_r.at[n], (ctx, mate))

    def to_group(n, d, src, dst):
        return remote(src, dst, tp_s.at[n, d], tp_r.at[n, d], (ctx, lax.rem(t + d, GROUPS)))

    def scatter(n, c, send, recv, d):
        part = pl.ds(2 * c, 2)
        return to_group(n + c, d, send.at[lax.rem(t + d, GROUPS), part], recv.at[t, part])

    def gather(n, c, send, recv, d):
        part = pl.ds(2 * c, 2)
        return to_group(n + c, d, send.at[lax.rem(lax.rem(t + d, GROUPS), 2), part], recv.at[t, part])

    order = (4, 3, 5, 2, 6, 1, 7)

    far = ring(z, 4)
    rows_near = [ring(z, k) for k in range(-3, 4)]

    def column(parity, slot):
        return lax.rem(y + RING - 2 - lax.rem(y + parity, 2) + 2 * slot, RING)

    def conv_fine(blocks):
        mine, swapped = [], []
        for slot, i in blocks:
            q, upper, lower = lax.div(column(core, slot), 2), lax.div(i, 2), lax.rem(i, 2)
            at = (2 * q + (i - 2 * q) * core, upper + (q - upper) * core, lower + (1 - lower) * core)
            mine.append(w2_all[at].astype(f32))
            swapped.append(w2_swap[q, upper, lower].astype(f32))
        mine, swapped = (jnp.concatenate(part, axis=0).astype(bf16) for part in (mine, swapped))
        sums = dot(mine, x2[0:L2]) + dot(swapped, x2[L2 : 2 * L2])
        for n, (slot, i) in enumerate(blocks):
            p2_send[i, slot] = sums[n * ROWS : (n + 1) * ROWS].astype(bf16)

    def fine_swap_done(last):
        @pl.when(core == 0)
        def _():
            for i in (far,) if last else rows_near:
                swap_one(1, i).wait_recv()

        @pl.when(core == 1)
        def _():
            for slot in (3,) if last else (0, 1, 2):
                swap_zero(1, column(1, slot)).wait_recv()

    def fine_copy(n, d, send, recv, index, slots):
        return to_group(n, d, send.at[index, slots], recv.at[t, slots])

    early, late, whole = pl.ds(0, 3), pl.ds(3, 1), pl.ds(0, 4)

    def fine_sums(last, act):
        for d in order:
            target = lax.rem(t + d, GROUPS)

            @pl.when(target != far)
            def _():
                act(fine_copy(2 + last, d, p2_send, p2_recv, target, late if last else early))

            if last:

                @pl.when(target == far)
                def _():
                    act(fine_copy(3, d, p2_send, p2_recv, target, whole))

    def fine_grads(last, act, source):
        for d in order:
            target = lax.rem(t + d, GROUPS)
            origin = ring(t, -d) if source else t

            @pl.when(origin != far)
            def _():
                act(fine_copy(4 + last, d, g_send, g_recv, lax.rem(target, 2), late if last else early))

            if last:

                @pl.when(origin == far)
                def _():
                    act(fine_copy(5, d, g_send, g_recv, lax.rem(target, 2), whole))

    def begun(copy):
        copy.start()

    def arrived(copy):
        copy.wait_recv()

    def left(copy):
        copy.wait_send()

    def with_taps(w, q, use):
        w_all, w_swap = taps[w]

        @pl.when(core == 0)
        def _():
            use([flat(w_all[2 * n]) for n in q], [flat(w_swap[n]) for n in q])

        @pl.when(core == 1)
        def _():
            use([flat(w_all[:, n, 1]) for n in q], [flat(w_swap[n]) for n in q])

    for d in (1, 7, 2, 6, 3, 5, 4):
        near(d).start()
    near_arrives(one + 1 - 2 * lax.rem(one, 2))
    second_start(0, 0)
    for n in (1, 2, 3):
        near_arrives(2 * piece(n))
        near_arrives(2 * piece(n) + 1)
        second_start(0, n)
    swap(0, two)
    for m in range(4):
        first(m).start()
    for side in (0, 1):
        halo(side).start()

    lane = iota((WIDE, 2 * LANES), 1)
    row = iota((WIDE, 2 * LANES), 0)
    half_lane = lax.rem(lane, LANES)
    pick = jnp.where(row == 2 * half_lane + 64 + lax.div(lane, LANES), 1.0, 0.0).astype(bf16)
    where_to = iota((RING * ROWS, FINE_C), 1)
    spread = jnp.where(
        iota((RING * ROWS, FINE_C), 0) == lax.div(where_to, OUT2) * ROWS + lax.rem(where_to, OUT2), 1.0, 0.0
    ).astype(bf16)
    at = ctx * POS + iota((1, LANES), 1) - EDGE
    inside = jnp.logical_and(at >= 0, at < count * POS)
    second_step(0, 1)
    for m in (2, 3):
        first(m, True).wait_recv()
    for m in (4, 5, 6):
        first(m).start()
    for side in (0, 1):
        halo(side).wait_recv()
        lanes = slice(0, 128) if side == 0 else slice(128 + FINE, WIDE)
        enc_wide[:, lanes] = edge_in[side]
        cot_wide[:, lanes] = shift(edge_in[side].astype(f32), 64, 1).astype(bf16)
    enc_ed = dot(enc_wide[...], pick)
    pooled = jnp.where(inside, (enc_ed[:, 0:LANES] + enc_ed[:, LANES:]) * 0.5, 0.0)
    pooled_own[...] = pooled.astype(bf16)
    pair(0, pooled_own, pooled_other).start()
    second_step(0, 2)
    enc_rows[...] = dot(spread, enc_ed.astype(bf16)).reshape(RING, ROWS, 2 * LANES).astype(bf16)
    cot_ed = dot(cot_wide[...], pick).astype(bf16)
    cot_rows[...] = dot(spread, cot_ed).reshape(RING, ROWS, 2 * LANES).astype(bf16)
    pair(0, pooled_own, pooled_other).wait_recv()
    for other, ref in enumerate((pooled_own, pooled_other)):
        value = ref[...].astype(f32)
        for k in range(5):
            start = other * L1 + k * FINE_C
            x1[start : start + FINE_C] = shift(value, 2 - k, 1).astype(bf16)
        x1[other * L1 + 880 : (other + 1) * L1] = jnp.zeros((16, LANES), bf16)
    for m in (0, 1, 4, 5, 6):
        first(m, True).wait_recv()
    second_step(0, 3)
    for n in range(4):
        second_start(1, n)
    swap(1, two)
    second_step(0, 4)

    for c in (0, 1):
        second_part(1, 1, 2 * c)
        second_part(1, 1, 2 * c + 1)
        if c == 0:
            swap_done(0)

        @pl.loop(2 * c, 2 * c + 2)
        def _(q):
            def use(mine, swapped):
                part = dot(mine[0], x1[0:L1]) + dot(swapped[0], x1[L1 : 2 * L1])
                p1_send[:, q] = part.reshape(RING, ROWS, LANES).astype(bf16)

            with_taps(0, [q], use)

        for d in order:
            scatter(0, c, p1_send, p1_recv, d).start()

    p1_recv[t] = p1_send[t]
    second_swap(1, 1)
    second_step(1, 2)
    for c in (0, 1):
        for d in order:
            scatter(0, c, p1_send, p1_recv, d).wait_recv()
    sides = [sum(p1_recv[2 * x + p].astype(f32) for x in range(4)) for p in (0, 1)]
    pre_c[...] = jnp.stack(sides, axis=1).reshape(COARSE_C, LANES)
    c_own[...] = jnp.where(inside, gelu_value(pre_c[...]), 0.0).astype(bf16)
    pair(1, c_own, c_other).start()
    slope_c[...] = gelu_slope(pre_c[...])
    pair(1, c_own, c_other).wait_recv()
    for other, ref in enumerate((c_own, c_other)):
        value = ref[...]
        wide = value.astype(f32)
        before, after = shift(wide, 1, 1).astype(bf16), shift(wide, -1, 1).astype(bf16)
        for start, even, odd in (
            (0, before, before),
            (192, value, value),
            (384, after, after),
            (640, before, value),
            (832, value, after),
        ):
            start += other * L2
            x2[start : start + COARSE_C, 0:LANES] = even
            x2[start : start + COARSE_C, LANES : 2 * LANES] = odd
        x2[other * L2 + 576 : other * L2 + 640] = jnp.zeros((64, 2 * LANES), bf16)
    second_step(1, 3)
    fine_swap_done(0)
    for slot in range(3):
        conv_fine([(slot, i) for i in rows_near])
    fine_sums(0, begun)
    second_step(1, 4)
    fine_swap_done(1)
    conv_fine([(slot, far) for slot in range(4)])
    conv_fine([(3, i) for i in rows_near])
    fine_sums(1, begun)
    p2_recv[t] = p2_send[t]

    def fine_slot(slot):
        for p in (0, 1):
            pre = sum(p2_recv[2 * x + p, slot].astype(f32) for x in range(4))
            value, slope = gelu_both(pre)
            at = column(p, slot)
            merged_rows[at] = (enc_rows[at].astype(f32) + value).astype(bf16)
            grad = (cot_rows[at].astype(f32) * slope).astype(bf16).astype(f32)
            even = jnp.where(inside, grad[:, 0:LANES], 0.0)
            odd = jnp.where(inside, grad[:, LANES:], 0.0)
            g_send[p, slot, :, 0:LANES] = (even + odd).astype(bf16)
            g_send[p, slot, :, LANES : 2 * LANES] = (even + shift(odd, 1, 1)).astype(bf16)

    @pl.when(t != far)
    def _():
        for d in order:
            fine_copy(2, d, p2_send, p2_recv, t, early).wait_recv()
        pl.loop(0, 3)(fine_slot)
        for d in order:
            fine_copy(4, d, g_send, g_recv, lax.rem(lax.rem(t + d, GROUPS), 2), early).start()
        for d in order:
            fine_copy(3, d, p2_send, p2_recv, t, late).wait_recv()

    @pl.when(t == far)
    def _():
        for d in order:
            fine_copy(3, d, p2_send, p2_recv, t, whole).wait_recv()
        pl.loop(0, 3)(fine_slot)

    fine_slot(3)
    fine_grads(1, begun, False)
    g_recv[t] = g_send[core]
    for side in (0, 1):
        halo(side).wait_send()
    for d in range(1, RING):
        near(d).wait_send()
    for m in range(7):
        first(m).wait_send()
    for w in (0, 1):
        for side in (0, 1):
            for n in range(4):
                for hop in (1, 2, 3, 4):
                    if hop < 4 or side == last_side(n):
                        second(w, side, hop, n).wait_send()
        swap_sent(w)
    pair(0, pooled_own, pooled_other).wait_send()
    pair(1, c_own, c_other).wait_send()
    for c in (0, 1):
        for d in order:
            scatter(0, c, p1_send, p1_recv, d).wait_send()
    back = iota((2 * LANES, FINE), 1)
    unpick = jnp.where(
        iota((2 * LANES, FINE), 0) == lax.rem(back, 2) * LANES + lax.div(back, 2) + EDGE, 1.0, 0.0
    ).astype(bf16)
    kept = dot_first(spread, flat(merged_rows[...])).astype(bf16)
    merged_ref[...] = dot(kept, unpick).astype(bf16)

    fine_grads(0, arrived, True)
    fine_grads(1, arrived, True)
    for c in (0, 1):
        columns = [lax.div(column(core, 2 * c + n), 2) for n in (0, 1)]
        block = jnp.concatenate([flat(g_recv[:, 2 * c + n]) for n in (0, 1)], axis=0)

        def add(mine, swapped):
            for other, use in enumerate((mine, swapped)):
                use = jnp.concatenate(use, axis=0)
                sums = dot_first(block[:, 0:LANES], use[:, 0:640])
                pairs = dot_first(block[:, LANES:], use[:, 640:1024])
                if c == 0:
                    y1[other], y2[other] = sums, pairs
                else:
                    y1[other] += sums
                    y2[other] += pairs

        with_taps(1, columns, add)

    def coarse_part(other):
        total = shift(y1[other, :, 0:192] + y2[other, :, 0:192], -1, 0)
        total = total + y1[other, :, 192:384] + y2[other, :, 192:384]
        total = total + shift(y1[other, :, 384:576], 1, 0)
        return transposed(total, COARSE_C)

    gc_out[...] = coarse_part(1)
    pair(2, gc_out, gc_in).start()
    own = coarse_part(0)
    pair(2, gc_out, gc_in).wait_recv()
    grad_c = jnp.where(inside, (own + gc_in[...]) * slope_c[...], 0.0).reshape(4, 2, ROWS, LANES).astype(bf16)
    gc_send[0] = grad_c[:, 0]
    gc_send[1] = grad_c[:, 1]
    for c in (0, 1):
        for d in order:
            gather(6, c, gc_send, gc_recv, d).start()
    gc_recv[t] = gc_send[core]
    pair(2, gc_out, gc_in).wait_send()
    for last in (0, 1):
        fine_sums(last, left)
        fine_grads(last, left, False)
    coarse_row = iota((LANES, FINE), 0)
    widen = jnp.where(coarse_row == lax.div(iota((LANES, FINE), 1), 2) + EDGE, 1.0, 0.0).astype(bf16)
    for c in (0, 1):
        for d in order:
            gather(6, c, gc_send, gc_recv, d).wait_recv()

        block = jnp.concatenate([flat(gc_recv[:, 2 * c + n]) for n in (0, 1)], axis=0)

        def add(mine, swapped):
            for other, use in enumerate((mine, swapped)):
                part = dot_first(block, jnp.concatenate(use, axis=0))
                if c == 0:
                    y4[other] = part
                else:
                    y4[other] += part

        with_taps(0, [2 * c, 2 * c + 1], add)

    def fine_part(other):
        total = None
        for k in range(5):
            term = shift(y4[other, :, k * FINE_C : (k + 1) * FINE_C], k - 2, 0)
            total = term if total is None else total + term
        return transposed(total, FINE_C)

    gp_out[...] = fine_part(1)
    pair(3, gp_out, gp_in).start()
    own = fine_part(0)
    for c in (0, 1):
        for d in order:
            gather(6, c, gc_send, gc_recv, d).wait_send()
    pair(3, gp_out, gp_in).wait_recv()
    total = (own + gp_in[...]) * 0.5
    high = total.astype(bf16)
    low = (total - high.astype(f32)).astype(bf16)
    genc_ref[...] = (cot_ref[...].astype(f32) + dot(high, widen) + dot(low, widen)).astype(bf16)

    pair(3, gp_out, gp_in).wait_send()


def shards(enc, w_down, w_up, cot):
    dma = pltpu.SemaphoreType.DMA
    vmem = pltpu.VMEM
    merged, grad_enc = pl.pallas_call(
        kernel,
        out_shape=[jax.ShapeDtypeStruct((FINE_C, FINE), bf16)] * 2,
        in_specs=[pl.BlockSpec(memory_space=vmem)] * 4,
        out_specs=[pl.BlockSpec(memory_space=vmem)] * 2,
        scratch_shapes=[
            vmem((2, FINE_C, 128), bf16),
            vmem((2, FINE_C, 128), bf16),
            vmem((FINE_C, WIDE), bf16),
            vmem((FINE_C, WIDE), bf16),
            vmem((RING, 4, 2, ROWS, L1), bf16),
            vmem((4, 4, 2, ROWS, L1), bf16),
            vmem((RING, 4, 2, ROWS, L2), bf16),
            vmem((4, 4, 2, ROWS, L2), bf16),
            vmem((FINE_C, LANES), bf16),
            vmem((FINE_C, LANES), bf16),
            vmem((2 * L1, LANES), bf16),
            vmem((GROUPS, 4, ROWS, LANES), bf16),
            vmem((GROUPS, 4, ROWS, LANES), bf16),
            vmem((COARSE_C, LANES), f32),
            vmem((COARSE_C, LANES), f32),
            vmem((COARSE_C, LANES), bf16),
            vmem((COARSE_C, LANES), bf16),
            vmem((2 * L2, 2 * LANES), bf16),
            vmem((RING, ROWS, 2 * LANES), bf16),
            vmem((RING, ROWS, 2 * LANES), bf16),
            vmem((RING, ROWS, 2 * LANES), bf16),
            vmem((GROUPS, 4, ROWS, 2 * LANES), bf16),
            vmem((GROUPS, 4, ROWS, 2 * LANES), bf16),
            vmem((2, 4, ROWS, 2 * LANES), bf16),
            vmem((GROUPS, 4, ROWS, 2 * LANES), bf16),
            vmem((2, LANES, 640), f32),
            vmem((2, LANES, 384), f32),
            vmem((COARSE_C, LANES), f32),
            vmem((COARSE_C, LANES), f32),
            vmem((2, 4, ROWS, LANES), bf16),
            vmem((GROUPS, 4, ROWS, LANES), bf16),
            vmem((2, LANES, L1), f32),
            vmem((FINE_C, LANES), f32),
            vmem((FINE_C, LANES), f32),
            dma((2,)),
            dma((2,)),
            dma((RING,)),
            dma((RING,)),
            dma((7,)),
            dma((7,)),
            dma((2, 2, 5, 4)),
            dma((2, 2, 5, 4)),
            dma((2, RING)),
            dma((2, RING)),
            dma((4,)),
            dma((4,)),
            dma((8, GROUPS)),
            dma((8, GROUPS)),
        ],
        compiler_params=pltpu.CompilerParams(
            collective_id=0, has_side_effects=True, vmem_limit_bytes=VMEM_LIMIT
        ),
    )(enc[0], cot[0], jnp.swapaxes(w_down, 1, 2), jnp.swapaxes(w_up, 1, 2))
    return merged[None], grad_enc[None]


def solution(mesh):
    placed = P(None, "tp", "ctx")
    return jax.shard_map(
        shards,
        mesh=mesh,
        in_specs=(placed,) * 4,
        out_specs=(placed, placed),
        check_vma=False,
    )
```

```python
import jax
import jax.numpy as jnp
from jax import lax
from jax.experimental import pallas as pl
from jax.experimental.pallas import tpu as pltpu
from jax.sharding import PartitionSpec as P

MESH = pl.DeviceIdType.MESH
bf16 = jnp.bfloat16
f32 = jnp.float32
root_half = 0.7071067811865476
norm_scale = 0.3989422804014327

RING = 8
GROUPS = 8
FINE_C, COARSE_C = 176, 192
OUT1, OUT2 = 24, 22
ROWS = 24
L1, L2 = 896, 1024
POS, LANES, EDGE = 192, 256, 32
FINE = 384
WIDE = 128 + FINE + 128
VMEM_LIMIT = 56 << 20


def erf(value):
    return lax.erf(value)


def gelu_value(value):
    return 0.5 * value * (1.0 + erf(value * root_half))


def gelu_both(value):
    cumulative = 0.5 * (1.0 + erf(value * root_half))
    return value * cumulative, cumulative + value * jnp.exp(-0.5 * value * value) * norm_scale


def gelu_slope(value):
    return gelu_both(value)[1]


def dot(a, b):
    return jnp.dot(a, b, preferred_element_type=f32)


def dot_first(a, b):
    return lax.dot_general(a, b, (((0,), (0,)), ((), ())), preferred_element_type=f32)


def iota(shape, dim):
    return lax.broadcasted_iota(jnp.int32, shape, dim)


def flat(block):
    lanes = block.shape[-1]
    return block.reshape(RING * ROWS, lanes)


def transposed(value, width):
    if width < LANES:
        value = jnp.concatenate([value, jnp.zeros((LANES, LANES - width), f32)], axis=1)
    return jnp.transpose(value)[:width]


def shift(value, amount, axis):
    size = value.shape[axis]
    return value if amount % size == 0 else pltpu.roll(value, amount % size, axis=axis)


def kernel(
    enc_in, cot_in, w1_in, w2_in, merged_ref, genc_ref, w1_ref, w2_ref,
    edge_out, edge_in, enc_wide, cot_wide, w1_all, w1_swap, w2_all, w2_swap,
    pooled_own, pooled_other, x1, p1_send, p1_recv, pre_c, slope_c, c_own, c_other, x2,
    enc_rows, cot_rows, merged_rows, p2_send, p2_recv, g_send, g_recv, y1, y2, gc_out, gc_in,
    gc_send, gc_recv, y4, gp_out, gp_in,
    in_s, halo_s, halo_r, near_s, near_r, first_s, first_r, second_s, second_r, swap_s, swap_r,
    pair_s, pair_r, tp_s, tp_r,
):
    own = slice(128, 128 + FINE)
    loads = [
        pltpu.make_async_copy(src, dst, in_s.at[n])
        for n, (src, dst) in enumerate(
            ((w1_in, w1_ref), (w2_in, w2_ref), (enc_in, enc_wide.at[:, own]), (cot_in, cot_wide.at[:, own]))
        )
    ]
    for load in loads:
        load.start()
    ctx, t = lax.axis_index("ctx"), lax.axis_index("tp")
    core = lax.rem(t, 2)
    mate = t + 1 - 2 * core
    z, y = lax.div(ctx, RING), lax.rem(ctx, RING)
    one = z + (y - z) * core
    two = y + (z - y) * core

    def ring(index, step):
        return lax.rem(index + RING + step, RING)

    def place(i, j):
        straight, crossed = i * RING + j, j * RING + i
        return straight + (crossed - straight) * core

    def remote(src, dst, send, recv, device):
        return pltpu.make_async_remote_copy(
            src_ref=src, dst_ref=dst, send_sem=send, recv_sem=recv, device_id=device, device_id_type=MESH
        )

    second_to = ((place(one, ring(two, 1)), t), (place(one, ring(two, -1)), t))
    count = RING * RING
    ctx_next, ctx_prev = lax.rem(ctx + 1, count), lax.rem(ctx + count - 1, count)

    barrier = pltpu.get_barrier_semaphore()
    partners = [(place(ring(one, d), two), t) for d in range(1, RING)]
    partners += [*second_to, (ctx_next, t), (ctx_prev, t)]
    partners += [(ctx, lax.rem(t + d, GROUPS)) for d in range(1, GROUPS)]
    for device in partners:
        pl.semaphore_signal(barrier, inc=1, device_id=device, device_id_type=MESH)

    for load in loads:
        load.wait()
    taps = ((w1_all, w1_swap), (w2_all, w2_swap))
    down = [w1_ref[k].astype(f32) for k in range(5)]
    up = [w2_ref[k].astype(f32) for k in range(5)]
    down = jnp.concatenate([*down, jnp.zeros((OUT1, 16), f32)], axis=1)
    up = jnp.concatenate([up[0], up[2], up[4], jnp.zeros((OUT2, 64), f32), up[1], up[3]], axis=1)
    up = jnp.concatenate([up, jnp.zeros((ROWS - OUT2, L2), f32)], axis=0)
    for w_all, block in ((w1_all, down), (w2_all, up)):
        w_all[two, lax.div(one, 2), lax.rem(one, 2)] = block.astype(bf16)
    low = iota((FINE_C, 128), 1) < 64
    last, first_tile = slice(FINE, 128 + FINE), slice(128, 256)
    enc_last, cot_last = enc_wide[:, last].astype(f32), shift(cot_wide[:, last].astype(f32), 64, 1)
    enc_first, cot_first = enc_wide[:, first_tile].astype(f32), shift(cot_wide[:, first_tile].astype(f32), 64, 1)
    edge_out[0] = jnp.where(low, cot_last, enc_last).astype(bf16)
    edge_out[1] = jnp.where(low, enc_first, cot_first).astype(bf16)
    pl.semaphore_wait(barrier, len(partners))

    def halo(side):
        to = ctx_next if side == 0 else ctx_prev
        return remote(edge_out.at[side], edge_in.at[side], halo_s.at[side], halo_r.at[side], (to, t))

    def near(d):
        block = w1_all.at[two, lax.div(one, 2), lax.rem(one, 2)]
        return remote(block, block, near_s.at[d], near_r.at[d], (place(ring(one, d), two), t))

    def near_arrives(j):
        d = ring(one, -j)
        block = w1_all.at[two, lax.div(j, 2), lax.rem(j, 2)]
        remote(block, block, near_s.at[d], near_r.at[d], (place(ring(one, d), two), t)).wait_recv()

    routes = ((0, 1), (0, -1), (0, 2), (0, -2), (-2, 1), (-2, 2), (2, -1))

    def first(m, arriving=False):
        origin, step = routes[m]
        index = ring(one, origin - step if arriving else origin)
        block = w2_all.at[two, lax.div(index, 2), lax.rem(index, 2)]
        return remote(block, block, first_s.at[m], first_r.at[m], (place(ring(one, step), two), t))

    def piece(n):
        return lax.rem(lax.div(one, 2) + (0, 1, 3, 2)[n], 4)

    def second(w, side, hop, n, arriving=False):
        step = hop if arriving else hop - 1
        index = ring(two, -step if side == 0 else step)
        block = taps[w][0].at[index, piece(n)]
        return remote(block, block, second_s.at[w, side, hop, n], second_r.at[w, side, hop, n], second_to[side])

    def swap_zero(w, index):
        return remote(
            taps[w][0].at[index], taps[w][1].at[lax.div(index, 2)],
            swap_s.at[w, lax.div(index, 2)], swap_r.at[w, lax.div(index, 2)], (ctx, mate),
        )

    def swap_one(w, index):
        return remote(
            taps[w][0].at[index, :, 0], taps[w][1].at[:, lax.div(index, 2), lax.rem(index, 2)],
            swap_s.at[w, index], swap_r.at[w, index], (ctx, mate),
        )

    def swap(w, index):
        @pl.when(jnp.logical_and(core == 0, lax.rem(index, 2) == 1))
        def _():
            swap_zero(w, index).start()

        @pl.when(core == 1)
        def _():
            swap_one(w, index).start()

    def swap_done(w):
        @pl.when(core == 0)
        def _():
            for index in range(RING):
                swap_one(w, index).wait_recv()

        @pl.when(core == 1)
        def _():
            for index in range(1, RING, 2):
                swap_zero(w, index).wait_recv()

    def swap_sent(w):
        @pl.when(core == 0)
        def _():
            for index in range(1, RING, 2):
                swap_zero(w, index).wait_send()

        @pl.when(core == 1)
        def _():
            for index in range(RING):
                swap_one(w, index).wait_send()

    def last_side(n):
        return 0 if n < 2 else 1

    def second_start(w, n):
        for side in (0, 1):
            second(w, side, 1, n).start()

    def second_part(w, hop, n):
        for side in (0, 1):
            second(w, side, hop, n, True).wait_recv()
            if hop < 3 or side == last_side(n):
                second(w, side, hop + 1, n).start()

    def second_swap(w, hop):
        swap(w, ring(two, hop))
        swap(w, ring(two, -hop))

    def second_step(w, hop):
        if hop < 4:
            for n in range(4):
                second_part(w, hop, n)
            second_swap(w, hop)
        else:
            for n in range(4):
                second(w, last_side(n), 4, n, True).wait_recv()
            swap(w, ring(two, 4))

    def pair(n, src, dst):
        return remote(src, dst, pair_s.at[n], pair_r.at[n], (ctx, mate))

    def to_group(n, d, src, dst):
        return remote(src, dst, tp_s.at[n, d], tp_r.at[n, d], (ctx, lax.rem(t + d, GROUPS)))

    def scatter(n, c, send, recv, d):
        part = pl.ds(2 * c, 2)
        return to_group(n + c, d, send.at[lax.rem(t + d, GROUPS), part], recv.at[t, part])

    def gather(n, c, send, recv, d):
        part = pl.ds(2 * c, 2)
        return to_group(n + c, d, send.at[lax.rem(lax.rem(t + d, GROUPS), 2), part], recv.at[t, part])

    order = (4, 3, 5, 2, 6, 1, 7)

    far = ring(z, 4)
    rows_near = [ring(z, k) for k in range(-3, 4)]

    def column(parity, slot):
        return lax.rem(y + RING - 2 - lax.rem(y + parity, 2) + 2 * slot, RING)

    def conv_fine(blocks):
        mine, swapped = [], []
        for slot, i in blocks:
            q, upper, lower = lax.div(column(core, slot), 2), lax.div(i, 2), lax.rem(i, 2)
            at = (2 * q + (i - 2 * q) * core, upper + (q - upper) * core, lower + (1 - lower) * core)
            mine.append(w2_all[at].astype(f32))
            swapped.append(w2_swap[q, upper, lower].astype(f32))
        mine, swapped = (jnp.concatenate(part, axis=0).astype(bf16) for part in (mine, swapped))
        sums = dot(mine, x2[0:L2]) + dot(swapped, x2[L2 : 2 * L2])
        for n, (slot, i) in enumerate(blocks):
            p2_send[i, slot] = sums[n * ROWS : (n + 1) * ROWS].astype(bf16)

    def fine_swap_done(last):
        @pl.when(core == 0)
        def _():
            for i in (far,) if last else rows_near:
                swap_one(1, i).wait_recv()

        @pl.when(core == 1)
        def _():
            for slot in (3,) if last else (0, 1, 2):
                swap_zero(1, column(1, slot)).wait_recv()

    def fine_copy(n, d, send, recv, index, slots):
        return to_group(n, d, send.at[index, slots], recv.at[t, slots])

    early, late, whole = pl.ds(0, 3), pl.ds(3, 1), pl.ds(0, 4)

    def fine_sums(last, act):
        for d in order:
            target = lax.rem(t + d, GROUPS)

            @pl.when(target != far)
            def _():
                act(fine_copy(2 + last, d, p2_send, p2_recv, target, late if last else early))

            if last:

                @pl.when(target == far)
                def _():
                    act(fine_copy(3, d, p2_send, p2_recv, target, whole))

    def fine_grads(last, act, source):
        for d in order:
            target = lax.rem(t + d, GROUPS)
            origin = ring(t, -d) if source else t

            @pl.when(origin != far)
            def _():
                act(fine_copy(4 + last, d, g_send, g_recv, lax.rem(target, 2), late if last else early))

            if last:

                @pl.when(origin == far)
                def _():
                    act(fine_copy(5, d, g_send, g_recv, lax.rem(target, 2), whole))

    def begun(copy):
        copy.start()

    def arrived(copy):
        copy.wait_recv()

    def left(copy):
        copy.wait_send()

    def own_taps(w, q, use):
        w_all = taps[w][0]

        @pl.when(core == 0)
        def _():
            use([flat(w_all[2 * n]) for n in q])

        @pl.when(core == 1)
        def _():
            use([flat(w_all[:, n, 1]) for n in q])

    for d in (1, 7, 2, 6, 3, 5, 4):
        near(d).start()
    near_arrives(one + 1 - 2 * lax.rem(one, 2))
    second_start(0, 0)
    for n in (1, 2, 3):
        near_arrives(2 * piece(n))
        near_arrives(2 * piece(n) + 1)
        second_start(0, n)
    swap(0, two)
    for m in range(4):
        first(m).start()
    for side in (0, 1):
        halo(side).start()

    lane = iota((WIDE, 2 * LANES), 1)
    row = iota((WIDE, 2 * LANES), 0)
    half_lane = lax.rem(lane, LANES)
    pick = jnp.where(row == 2 * half_lane + 64 + lax.div(lane, LANES), 1.0, 0.0).astype(bf16)
    where_to = iota((RING * ROWS, FINE_C), 1)
    spread = jnp.where(
        iota((RING * ROWS, FINE_C), 0) == lax.div(where_to, OUT2) * ROWS + lax.rem(where_to, OUT2), 1.0, 0.0
    ).astype(bf16)
    at = ctx * POS + iota((1, LANES), 1) - EDGE
    inside = jnp.logical_and(at >= 0, at < count * POS)
    second_step(0, 1)
    for m in (2, 3):
        first(m, True).wait_recv()
    for m in (4, 5, 6):
        first(m).start()
    for side in (0, 1):
        halo(side).wait_recv()
        lanes = slice(0, 128) if side == 0 else slice(128 + FINE, WIDE)
        enc_wide[:, lanes] = edge_in[side]
        cot_wide[:, lanes] = shift(edge_in[side].astype(f32), 64, 1).astype(bf16)
    enc_ed = dot(enc_wide[...], pick)
    pooled = jnp.where(inside, (enc_ed[:, 0:LANES] + enc_ed[:, LANES:]) * 0.5, 0.0)
    pooled_own[...] = pooled.astype(bf16)
    pair(0, pooled_own, pooled_other).start()
    second_step(0, 2)
    enc_rows[...] = dot(spread, enc_ed.astype(bf16)).reshape(RING, ROWS, 2 * LANES).astype(bf16)
    cot_ed = dot(cot_wide[...], pick).astype(bf16)
    cot_rows[...] = dot(spread, cot_ed).reshape(RING, ROWS, 2 * LANES).astype(bf16)
    pair(0, pooled_own, pooled_other).wait_recv()
    for other, ref in enumerate((pooled_own, pooled_other)):
        value = ref[...].astype(f32)
        for k in range(5):
            start = other * L1 + k * FINE_C
            x1[start : start + FINE_C] = shift(value, 2 - k, 1).astype(bf16)
        x1[other * L1 + 880 : (other + 1) * L1] = jnp.zeros((16, LANES), bf16)
    for m in (0, 1, 4, 5, 6):
        first(m, True).wait_recv()
    second_step(0, 3)
    for n in range(4):
        second_start(1, n)
    swap(1, two)
    second_step(0, 4)

    for c in (0, 1):
        second_part(1, 1, 2 * c)
        second_part(1, 1, 2 * c + 1)
        if c == 0:
            swap_done(0)

        @pl.loop(2 * c, 2 * c + 2)
        def _(q):
            swapped = dot(flat(w1_swap[q]), x1[L1 : 2 * L1])

            def use(mine):
                part = dot(mine[0], x1[0:L1]) + swapped
                p1_send[:, q] = part.reshape(RING, ROWS, LANES).astype(bf16)

            own_taps(0, [q], use)

        for d in order:
            scatter(0, c, p1_send, p1_recv, d).start()

    p1_recv[t] = p1_send[t]
    second_swap(1, 1)
    second_step(1, 2)
    for c in (0, 1):
        for d in order:
            scatter(0, c, p1_send, p1_recv, d).wait_recv()
    sides = [sum(p1_recv[2 * x + p].astype(f32) for x in range(4)) for p in (0, 1)]
    pre_c[...] = jnp.stack(sides, axis=1).reshape(COARSE_C, LANES)
    c_own[...] = jnp.where(inside, gelu_value(pre_c[...]), 0.0).astype(bf16)
    pair(1, c_own, c_other).start()
    slope_c[...] = gelu_slope(pre_c[...])
    pair(1, c_own, c_other).wait_recv()
    for other, ref in enumerate((c_own, c_other)):
        value = ref[...]
        wide = value.astype(f32)
        before, after = shift(wide, 1, 1).astype(bf16), shift(wide, -1, 1).astype(bf16)
        for start, even, odd in (
            (0, before, before),
            (192, value, value),
            (384, after, after),
            (640, before, value),
            (832, value, after),
        ):
            start += other * L2
            x2[start : start + COARSE_C, 0:LANES] = even
            x2[start : start + COARSE_C, LANES : 2 * LANES] = odd
        x2[other * L2 + 576 : other * L2 + 640] = jnp.zeros((64, 2 * LANES), bf16)
    second_step(1, 3)
    fine_swap_done(0)
    for slot in range(3):
        conv_fine([(slot, i) for i in rows_near])
    fine_sums(0, begun)
    second_step(1, 4)
    fine_swap_done(1)
    conv_fine([(slot, far) for slot in range(4)])
    conv_fine([(3, i) for i in rows_near])
    fine_sums(1, begun)
    p2_recv[t] = p2_send[t]

    def fine_slot(slot):
        for p in (0, 1):
            pre = sum(p2_recv[2 * x + p, slot].astype(f32) for x in range(4))
            value, slope = gelu_both(pre)
            at = column(p, slot)
            merged_rows[at] = (enc_rows[at].astype(f32) + value).astype(bf16)
            grad = (cot_rows[at].astype(f32) * slope).astype(bf16).astype(f32)
            even = jnp.where(inside, grad[:, 0:LANES], 0.0)
            odd = jnp.where(inside, grad[:, LANES:], 0.0)
            g_send[p, slot, :, 0:LANES] = (even + odd).astype(bf16)
            g_send[p, slot, :, LANES : 2 * LANES] = (even + shift(odd, 1, 1)).astype(bf16)

    @pl.when(t != far)
    def _():
        for d in order:
            fine_copy(2, d, p2_send, p2_recv, t, early).wait_recv()
        pl.loop(0, 3)(fine_slot)
        for d in order:
            fine_copy(4, d, g_send, g_recv, lax.rem(lax.rem(t + d, GROUPS), 2), early).start()
        for d in order:
            fine_copy(3, d, p2_send, p2_recv, t, late).wait_recv()

    @pl.when(t == far)
    def _():
        for d in order:
            fine_copy(3, d, p2_send, p2_recv, t, whole).wait_recv()
        pl.loop(0, 3)(fine_slot)

    fine_slot(3)
    fine_grads(1, begun, False)
    g_recv[t] = g_send[core]
    for side in (0, 1):
        halo(side).wait_send()
    for d in range(1, RING):
        near(d).wait_send()
    for m in range(7):
        first(m).wait_send()
    for w in (0, 1):
        for side in (0, 1):
            for n in range(4):
                for hop in (1, 2, 3, 4):
                    if hop < 4 or side == last_side(n):
                        second(w, side, hop, n).wait_send()
        swap_sent(w)
    pair(0, pooled_own, pooled_other).wait_send()
    pair(1, c_own, c_other).wait_send()
    for c in (0, 1):
        for d in order:
            scatter(0, c, p1_send, p1_recv, d).wait_send()
    back = iota((2 * LANES, FINE), 1)
    unpick = jnp.where(
        iota((2 * LANES, FINE), 0) == lax.rem(back, 2) * LANES + lax.div(back, 2) + EDGE, 1.0, 0.0
    ).astype(bf16)
    kept = dot_first(spread, flat(merged_rows[...])).astype(bf16)
    merged_ref[...] = dot(kept, unpick).astype(bf16)

    fine_grads(0, arrived, True)
    fine_grads(1, arrived, True)
    columns = [lax.div(column(core, slot), 2) for slot in range(4)]
    block = jnp.concatenate([flat(g_recv[:, slot]) for slot in range(4)], axis=0)

    def back_fine(other, use):
        use = jnp.concatenate(use, axis=0)
        y1[other] = dot_first(block[:, 0:LANES], use[:, 0:640])
        y2[other] = dot_first(block[:, LANES:], use[:, 640:1024])

    back_fine(1, [flat(w2_swap[n]) for n in columns])

    def coarse_part(other):
        total = shift(y1[other, :, 0:192] + y2[other, :, 0:192], -1, 0)
        total = total + y1[other, :, 192:384] + y2[other, :, 192:384]
        total = total + shift(y1[other, :, 384:576], 1, 0)
        return transposed(total, COARSE_C)

    gc_out[...] = coarse_part(1)
    pair(2, gc_out, gc_in).start()
    own_taps(1, columns, lambda use: back_fine(0, use))
    own = coarse_part(0)
    pair(2, gc_out, gc_in).wait_recv()
    grad_c = jnp.where(inside, (own + gc_in[...]) * slope_c[...], 0.0).reshape(4, 2, ROWS, LANES).astype(bf16)
    gc_send[0] = grad_c[:, 0]
    gc_send[1] = grad_c[:, 1]
    for c in (0, 1):
        for d in order:
            gather(6, c, gc_send, gc_recv, d).start()
    gc_recv[t] = gc_send[core]
    pair(2, gc_out, gc_in).wait_send()
    for last in (0, 1):
        fine_sums(last, left)
        fine_grads(last, left, False)
    coarse_row = iota((LANES, FINE), 0)
    widen = jnp.where(coarse_row == lax.div(iota((LANES, FINE), 1), 2) + EDGE, 1.0, 0.0).astype(bf16)
    for c in (0, 1):
        for d in order:
            gather(6, c, gc_send, gc_recv, d).wait_recv()

        coarse_block = jnp.concatenate([flat(gc_recv[:, 2 * c + n]) for n in (0, 1)], axis=0)
        pair_of = [2 * c, 2 * c + 1]

        def back_coarse(other, use, c=c, coarse_block=coarse_block):
            part = dot_first(coarse_block, jnp.concatenate(use, axis=0))
            if c == 0:
                y4[other] = part
            else:
                y4[other] += part

        back_coarse(1, [flat(w1_swap[n]) for n in pair_of])
        if c == 0:
            own_taps(0, pair_of, lambda use: back_coarse(0, use))

    def fine_part(other):
        total = None
        for k in range(5):
            term = shift(y4[other, :, k * FINE_C : (k + 1) * FINE_C], k - 2, 0)
            total = term if total is None else total + term
        return transposed(total, FINE_C)

    gp_out[...] = fine_part(1)
    pair(3, gp_out, gp_in).start()
    own_taps(0, pair_of, lambda use: back_coarse(0, use))
    own = fine_part(0)
    for c in (0, 1):
        for d in order:
            gather(6, c, gc_send, gc_recv, d).wait_send()
    pair(3, gp_out, gp_in).wait_recv()
    total = (own + gp_in[...]) * 0.5
    high = total.astype(bf16)
    low = (total - high.astype(f32)).astype(bf16)
    genc_ref[...] = (cot_wide[:, 128 : 128 + FINE].astype(f32) + dot(high, widen) + dot(low, widen)).astype(bf16)

    pair(3, gp_out, gp_in).wait_send()


def shards(enc, w_down, w_up, cot):
    dma = pltpu.SemaphoreType.DMA
    vmem = pltpu.VMEM
    merged, grad_enc = pl.pallas_call(
        kernel,
        out_shape=[jax.ShapeDtypeStruct((FINE_C, FINE), bf16)] * 2,
        in_specs=[pl.BlockSpec(memory_space=pltpu.HBM)] * 4,
        out_specs=[pl.BlockSpec(memory_space=vmem)] * 2,
        scratch_shapes=[
            vmem((5, OUT1, FINE_C), bf16),
            vmem((5, OUT2, COARSE_C), bf16),
            vmem((2, FINE_C, 128), bf16),
            vmem((2, FINE_C, 128), bf16),
            vmem((FINE_C, WIDE), bf16),
            vmem((FINE_C, WIDE), bf16),
            vmem((RING, 4, 2, ROWS, L1), bf16),
            vmem((4, 4, 2, ROWS, L1), bf16),
            vmem((RING, 4, 2, ROWS, L2), bf16),
            vmem((4, 4, 2, ROWS, L2), bf16),
            vmem((FINE_C, LANES), bf16),
            vmem((FINE_C, LANES), bf16),
            vmem((2 * L1, LANES), bf16),
            vmem((GROUPS, 4, ROWS, LANES), bf16),
            vmem((GROUPS, 4, ROWS, LANES), bf16),
            vmem((COARSE_C, LANES), f32),
            vmem((COARSE_C, LANES), f32),
            vmem((COARSE_C, LANES), bf16),
            vmem((COARSE_C, LANES), bf16),
            vmem((2 * L2, 2 * LANES), bf16),
            vmem((RING, ROWS, 2 * LANES), bf16),
            vmem((RING, ROWS, 2 * LANES), bf16),
            vmem((RING, ROWS, 2 * LANES), bf16),
            vmem((GROUPS, 4, ROWS, 2 * LANES), bf16),
            vmem((GROUPS, 4, ROWS, 2 * LANES), bf16),
            vmem((2, 4, ROWS, 2 * LANES), bf16),
            vmem((GROUPS, 4, ROWS, 2 * LANES), bf16),
            vmem((2, LANES, 640), f32),
            vmem((2, LANES, 384), f32),
            vmem((COARSE_C, LANES), f32),
            vmem((COARSE_C, LANES), f32),
            vmem((2, 4, ROWS, LANES), bf16),
            vmem((GROUPS, 4, ROWS, LANES), bf16),
            vmem((2, LANES, L1), f32),
            vmem((FINE_C, LANES), f32),
            vmem((FINE_C, LANES), f32),
            dma((4,)),
            dma((2,)),
            dma((2,)),
            dma((RING,)),
            dma((RING,)),
            dma((7,)),
            dma((7,)),
            dma((2, 2, 5, 4)),
            dma((2, 2, 5, 4)),
            dma((2, RING)),
            dma((2, RING)),
            dma((4,)),
            dma((4,)),
            dma((8, GROUPS)),
            dma((8, GROUPS)),
        ],
        compiler_params=pltpu.CompilerParams(
            collective_id=0, has_side_effects=True, vmem_limit_bytes=VMEM_LIMIT
        ),
    )(enc[0], cot[0], jnp.swapaxes(w_down, 1, 2), jnp.swapaxes(w_up, 1, 2))
    return merged[None], grad_enc[None]


def solution(mesh):
    placed = P(None, "tp", "ctx")
    return jax.shard_map(
        shards,
        mesh=mesh,
        in_specs=(placed,) * 4,
        out_specs=(placed, placed),
        check_vma=False,
    )
```

```python
import jax
import jax.numpy as jnp
from jax import lax
from jax.experimental import pallas as pl
from jax.experimental.pallas import tpu as pltpu
from jax.sharding import PartitionSpec as P

MESH = pl.DeviceIdType.MESH
bf16 = jnp.bfloat16
f32 = jnp.float32
root_half = 0.7071067811865476
norm_scale = 0.3989422804014327

RING = 8
GROUPS = 8
FINE_C, COARSE_C = 176, 192
OUT1, OUT2 = 24, 22
ROWS = 24
L1, L2 = 896, 1024
POS, LANES, EDGE = 192, 256, 32
FINE = 384
WIDE = 128 + FINE + 128
VMEM_LIMIT = 56 << 20


def erf(value):
    return lax.erf(value)


def gelu_value(value):
    return 0.5 * value * (1.0 + erf(value * root_half))


def gelu_both(value):
    cumulative = 0.5 * (1.0 + erf(value * root_half))
    return value * cumulative, cumulative + value * jnp.exp(-0.5 * value * value) * norm_scale


def gelu_slope(value):
    return gelu_both(value)[1]


def dot(a, b):
    return jnp.dot(a, b, preferred_element_type=f32)


def dot_first(a, b):
    return lax.dot_general(a, b, (((0,), (0,)), ((), ())), preferred_element_type=f32)


def iota(shape, dim):
    return lax.broadcasted_iota(jnp.int32, shape, dim)


def flat(block):
    lanes = block.shape[-1]
    return block.reshape(RING * ROWS, lanes)


def transposed(value, width):
    if width < LANES:
        value = jnp.concatenate([value, jnp.zeros((LANES, LANES - width), f32)], axis=1)
    return jnp.transpose(value)[:width]


def shift(value, amount, axis):
    size = value.shape[axis]
    return value if amount % size == 0 else pltpu.roll(value, amount % size, axis=axis)


def kernel(
    enc_in, cot_in, w1_in, w2_in, out_ref, w1_ref, w2_ref,
    edge_out, edge_in, enc_wide, cot_wide, w1_all, w1_swap, w2_all, w2_swap,
    pooled_own, pooled_other, x1, p1_send, p1_recv, pre_c, slope_c, c_own, c_other, x2,
    enc_rows, cot_rows, merged_rows, p2_send, p2_recv, g_send, g_recv, y1, y2, gc_out, gc_in,
    gc_send, gc_recv, y4, gp_out, gp_in,
    in_s, halo_s, halo_r, near_s, near_r, first_s, first_r, second_s, second_r, swap_s, swap_r,
    pair_s, pair_r, tp_s, tp_r,
):
    own = slice(128, 128 + FINE)
    loads = [
        pltpu.make_async_copy(src, dst, in_s.at[n])
        for n, (src, dst) in enumerate(
            ((w1_in, w1_ref), (w2_in, w2_ref), (enc_in, enc_wide.at[:, own]), (cot_in, cot_wide.at[:, own]))
        )
    ]
    for load in loads:
        load.start()
    ctx, t = lax.axis_index("ctx"), lax.axis_index("tp")
    core = lax.rem(t, 2)
    mate = t + 1 - 2 * core
    z, y = lax.div(ctx, RING), lax.rem(ctx, RING)
    one = z + (y - z) * core
    two = y + (z - y) * core

    def ring(index, step):
        return lax.rem(index + RING + step, RING)

    def place(i, j):
        straight, crossed = i * RING + j, j * RING + i
        return straight + (crossed - straight) * core

    def remote(src, dst, send, recv, device):
        return pltpu.make_async_remote_copy(
            src_ref=src, dst_ref=dst, send_sem=send, recv_sem=recv, device_id=device, device_id_type=MESH
        )

    second_to = ((place(one, ring(two, 1)), t), (place(one, ring(two, -1)), t))
    count = RING * RING
    ctx_next, ctx_prev = lax.rem(ctx + 1, count), lax.rem(ctx + count - 1, count)

    barrier = pltpu.get_barrier_semaphore()
    partners = [(place(ring(one, d), two), t) for d in range(1, RING)]
    partners += [*second_to, (ctx_next, t), (ctx_prev, t)]
    partners += [(ctx, lax.rem(t + d, GROUPS)) for d in range(1, GROUPS)]
    for device in partners:
        pl.semaphore_signal(barrier, inc=1, device_id=device, device_id_type=MESH)

    for load in loads:
        load.wait()
    taps = ((w1_all, w1_swap), (w2_all, w2_swap))
    down = [w1_ref[k].astype(f32) for k in range(5)]
    up = [w2_ref[k].astype(f32) for k in range(5)]
    down = jnp.concatenate([*down, jnp.zeros((OUT1, 16), f32)], axis=1)
    up = jnp.concatenate([up[0], up[2], up[4], jnp.zeros((OUT2, 64), f32), up[1], up[3]], axis=1)
    up = jnp.concatenate([up, jnp.zeros((ROWS - OUT2, L2), f32)], axis=0)
    for w_all, block in ((w1_all, down), (w2_all, up)):
        w_all[two, lax.div(one, 2), lax.rem(one, 2)] = block.astype(bf16)
    low = iota((FINE_C, 128), 1) < 64
    last, first_tile = slice(FINE, 128 + FINE), slice(128, 256)
    enc_last, cot_last = enc_wide[:, last].astype(f32), shift(cot_wide[:, last].astype(f32), 64, 1)
    enc_first, cot_first = enc_wide[:, first_tile].astype(f32), shift(cot_wide[:, first_tile].astype(f32), 64, 1)
    edge_out[0] = jnp.where(low, cot_last, enc_last).astype(bf16)
    edge_out[1] = jnp.where(low, enc_first, cot_first).astype(bf16)
    pl.semaphore_wait(barrier, len(partners))

    def halo(side):
        to = ctx_next if side == 0 else ctx_prev
        return remote(edge_out.at[side], edge_in.at[side], halo_s.at[side], halo_r.at[side], (to, t))

    def near(d):
        block = w1_all.at[two, lax.div(one, 2), lax.rem(one, 2)]
        return remote(block, block, near_s.at[d], near_r.at[d], (place(ring(one, d), two), t))

    def near_arrives(j):
        d = ring(one, -j)
        block = w1_all.at[two, lax.div(j, 2), lax.rem(j, 2)]
        remote(block, block, near_s.at[d], near_r.at[d], (place(ring(one, d), two), t)).wait_recv()

    routes = ((0, 1), (0, -1), (0, 2), (0, -2), (-2, 1), (-2, 2), (2, -1))

    def first(m, arriving=False):
        origin, step = routes[m]
        index = ring(one, origin - step if arriving else origin)
        block = w2_all.at[two, lax.div(index, 2), lax.rem(index, 2)]
        return remote(block, block, first_s.at[m], first_r.at[m], (place(ring(one, step), two), t))

    def piece(n):
        return lax.rem(lax.div(one, 2) + (0, 1, 3, 2)[n], 4)

    def second(w, side, hop, n, arriving=False):
        step = hop if arriving else hop - 1
        index = ring(two, -step if side == 0 else step)
        block = taps[w][0].at[index, piece(n)]
        return remote(block, block, second_s.at[w, side, hop, n], second_r.at[w, side, hop, n], second_to[side])

    def swap_zero(w, index):
        return remote(
            taps[w][0].at[index], taps[w][1].at[lax.div(index, 2)],
            swap_s.at[w, lax.div(index, 2)], swap_r.at[w, lax.div(index, 2)], (ctx, mate),
        )

    def swap_one(w, index):
        return remote(
            taps[w][0].at[index, :, 0], taps[w][1].at[:, lax.div(index, 2), lax.rem(index, 2)],
            swap_s.at[w, index], swap_r.at[w, index], (ctx, mate),
        )

    def swap(w, index):
        @pl.when(jnp.logical_and(core == 0, lax.rem(index, 2) == 1))
        def _():
            swap_zero(w, index).start()

        @pl.when(core == 1)
        def _():
            swap_one(w, index).start()

    def swap_done(w):
        @pl.when(core == 0)
        def _():
            for index in range(RING):
                swap_one(w, index).wait_recv()

        @pl.when(core == 1)
        def _():
            for index in range(1, RING, 2):
                swap_zero(w, index).wait_recv()

    def swap_sent(w):
        @pl.when(core == 0)
        def _():
            for index in range(1, RING, 2):
                swap_zero(w, index).wait_send()

        @pl.when(core == 1)
        def _():
            for index in range(RING):
                swap_one(w, index).wait_send()

    def last_side(n):
        return 0 if n < 2 else 1

    def second_start(w, n):
        for side in (0, 1):
            second(w, side, 1, n).start()

    def second_part(w, hop, n):
        for side in (0, 1):
            second(w, side, hop, n, True).wait_recv()
            if hop < 3 or side == last_side(n):
                second(w, side, hop + 1, n).start()

    def second_swap(w, hop):
        swap(w, ring(two, hop))
        swap(w, ring(two, -hop))

    def second_step(w, hop):
        if hop < 4:
            for n in range(4):
                second_part(w, hop, n)
            second_swap(w, hop)
        else:
            for n in range(4):
                second(w, last_side(n), 4, n, True).wait_recv()
            swap(w, ring(two, 4))

    def pair(n, src, dst):
        return remote(src, dst, pair_s.at[n], pair_r.at[n], (ctx, mate))

    def to_group(n, d, src, dst):
        return remote(src, dst, tp_s.at[n, d], tp_r.at[n, d], (ctx, lax.rem(t + d, GROUPS)))

    def scatter(n, c, send, recv, d):
        part = pl.ds(2 * c, 2)
        return to_group(n + c, d, send.at[lax.rem(t + d, GROUPS), part], recv.at[t, part])

    def gather(n, c, send, recv, d):
        part = pl.ds(2 * c, 2)
        return to_group(n + c, d, send.at[lax.rem(lax.rem(t + d, GROUPS), 2), part], recv.at[t, part])

    order = (4, 3, 5, 2, 6, 1, 7)

    far = ring(z, 4)
    rows_near = [ring(z, k) for k in range(-3, 4)]

    def column(parity, slot):
        return lax.rem(y + RING - 2 - lax.rem(y + parity, 2) + 2 * slot, RING)

    def conv_fine(blocks):
        mine, swapped = [], []
        for slot, i in blocks:
            q, upper, lower = lax.div(column(core, slot), 2), lax.div(i, 2), lax.rem(i, 2)
            at = (2 * q + (i - 2 * q) * core, upper + (q - upper) * core, lower + (1 - lower) * core)
            mine.append(w2_all[at].astype(f32))
            swapped.append(w2_swap[q, upper, lower].astype(f32))
        mine, swapped = (jnp.concatenate(part, axis=0).astype(bf16) for part in (mine, swapped))
        sums = dot(mine, x2[0:L2]) + dot(swapped, x2[L2 : 2 * L2])
        for n, (slot, i) in enumerate(blocks):
            p2_send[i, slot] = sums[n * ROWS : (n + 1) * ROWS].astype(bf16)

    def fine_swap_done(last):
        @pl.when(core == 0)
        def _():
            for i in (far,) if last else rows_near:
                swap_one(1, i).wait_recv()

        @pl.when(core == 1)
        def _():
            for slot in (3,) if last else (0, 1, 2):
                swap_zero(1, column(1, slot)).wait_recv()

    def fine_copy(n, d, send, recv, index, slots):
        return to_group(n, d, send.at[index, slots], recv.at[t, slots])

    early, late, whole = pl.ds(0, 3), pl.ds(3, 1), pl.ds(0, 4)

    def fine_sums(last, act):
        for d in order:
            target = lax.rem(t + d, GROUPS)

            @pl.when(target != far)
            def _():
                act(fine_copy(2 + last, d, p2_send, p2_recv, target, late if last else early))

            if last:

                @pl.when(target == far)
                def _():
                    act(fine_copy(3, d, p2_send, p2_recv, target, whole))

    def fine_grads(last, act, source):
        for d in order:
            target = lax.rem(t + d, GROUPS)
            origin = ring(t, -d) if source else t

            @pl.when(origin != far)
            def _():
                act(fine_copy(4 + last, d, g_send, g_recv, lax.rem(target, 2), late if last else early))

            if last:

                @pl.when(origin == far)
                def _():
                    act(fine_copy(5, d, g_send, g_recv, lax.rem(target, 2), whole))

    def begun(copy):
        copy.start()

    def arrived(copy):
        copy.wait_recv()

    def left(copy):
        copy.wait_send()

    def own_taps(w, q, use):
        w_all = taps[w][0]

        @pl.when(core == 0)
        def _():
            use([flat(w_all[2 * n]) for n in q])

        @pl.when(core == 1)
        def _():
            use([flat(w_all[:, n, 1]) for n in q])

    for d in (1, 7, 2, 6, 3, 5, 4):
        near(d).start()
    near_arrives(one + 1 - 2 * lax.rem(one, 2))
    second_start(0, 0)
    for n in (1, 2, 3):
        near_arrives(2 * piece(n))
        near_arrives(2 * piece(n) + 1)
        second_start(0, n)
    swap(0, two)
    for m in range(4):
        first(m).start()
    for side in (0, 1):
        halo(side).start()

    lane = iota((WIDE, 2 * LANES), 1)
    row = iota((WIDE, 2 * LANES), 0)
    half_lane = lax.rem(lane, LANES)
    pick = jnp.where(row == 2 * half_lane + 64 + lax.div(lane, LANES), 1.0, 0.0).astype(bf16)
    where_to = iota((RING * ROWS, FINE_C), 1)
    spread = jnp.where(
        iota((RING * ROWS, FINE_C), 0) == lax.div(where_to, OUT2) * ROWS + lax.rem(where_to, OUT2), 1.0, 0.0
    ).astype(bf16)
    at = ctx * POS + iota((1, LANES), 1) - EDGE
    inside = jnp.logical_and(at >= 0, at < count * POS)
    second_step(0, 1)
    for m in (2, 3):
        first(m, True).wait_recv()
    for m in (4, 5, 6):
        first(m).start()
    for side in (0, 1):
        halo(side).wait_recv()
        lanes = slice(0, 128) if side == 0 else slice(128 + FINE, WIDE)
        enc_wide[:, lanes] = edge_in[side]
        cot_wide[:, lanes] = shift(edge_in[side].astype(f32), 64, 1).astype(bf16)
    enc_ed = dot(enc_wide[...], pick)
    pooled = jnp.where(inside, (enc_ed[:, 0:LANES] + enc_ed[:, LANES:]) * 0.5, 0.0)
    pooled_own[...] = pooled.astype(bf16)
    pair(0, pooled_own, pooled_other).start()
    second_step(0, 2)
    enc_rows[...] = dot(spread, enc_ed.astype(bf16)).reshape(RING, ROWS, 2 * LANES).astype(bf16)
    cot_ed = dot(cot_wide[...], pick).astype(bf16)
    cot_rows[...] = dot(spread, cot_ed).reshape(RING, ROWS, 2 * LANES).astype(bf16)
    pair(0, pooled_own, pooled_other).wait_recv()
    for other, ref in enumerate((pooled_own, pooled_other)):
        value = ref[...].astype(f32)
        for k in range(5):
            start = other * L1 + k * FINE_C
            x1[start : start + FINE_C] = shift(value, 2 - k, 1).astype(bf16)
        x1[other * L1 + 880 : (other + 1) * L1] = jnp.zeros((16, LANES), bf16)
    for m in (0, 1, 4, 5, 6):
        first(m, True).wait_recv()
    second_step(0, 3)
    for n in range(4):
        second_start(1, n)
    swap(1, two)
    second_step(0, 4)

    for c in (0, 1):
        second_part(1, 1, 2 * c)
        second_part(1, 1, 2 * c + 1)
        if c == 0:
            swap_done(0)

        @pl.loop(2 * c, 2 * c + 2)
        def _(q):
            swapped = dot(flat(w1_swap[q]), x1[L1 : 2 * L1])

            def use(mine):
                part = dot(mine[0], x1[0:L1]) + swapped
                p1_send[:, q] = part.reshape(RING, ROWS, LANES).astype(bf16)

            own_taps(0, [q], use)

        for d in order:
            scatter(0, c, p1_send, p1_recv, d).start()

    p1_recv[t] = p1_send[t]
    second_swap(1, 1)
    second_step(1, 2)
    for c in (0, 1):
        for d in order:
            scatter(0, c, p1_send, p1_recv, d).wait_recv()
    sides = [sum(p1_recv[2 * x + p].astype(f32) for x in range(4)) for p in (0, 1)]
    pre_c[...] = jnp.stack(sides, axis=1).reshape(COARSE_C, LANES)
    c_own[...] = jnp.where(inside, gelu_value(pre_c[...]), 0.0).astype(bf16)
    pair(1, c_own, c_other).start()
    slope_c[...] = gelu_slope(pre_c[...])
    pair(1, c_own, c_other).wait_recv()
    for other, ref in enumerate((c_own, c_other)):
        value = ref[...]
        wide = value.astype(f32)
        before, after = shift(wide, 1, 1).astype(bf16), shift(wide, -1, 1).astype(bf16)
        for start, even, odd in (
            (0, before, before),
            (192, value, value),
            (384, after, after),
            (640, before, value),
            (832, value, after),
        ):
            start += other * L2
            x2[start : start + COARSE_C, 0:LANES] = even
            x2[start : start + COARSE_C, LANES : 2 * LANES] = odd
        x2[other * L2 + 576 : other * L2 + 640] = jnp.zeros((64, 2 * LANES), bf16)
    second_step(1, 3)
    fine_swap_done(0)
    conv_fine([(slot, i) for slot in range(3) for i in rows_near])
    fine_sums(0, begun)
    second_step(1, 4)
    fine_swap_done(1)
    conv_fine([(slot, far) for slot in range(4)] + [(3, i) for i in rows_near])
    fine_sums(1, begun)
    p2_recv[t] = p2_send[t]

    def fine_slot(slot):
        for p in (0, 1):
            pre = sum(p2_recv[2 * x + p, slot].astype(f32) for x in range(4))
            value, slope = gelu_both(pre)
            at = column(p, slot)
            merged_rows[at] = (enc_rows[at].astype(f32) + value).astype(bf16)
            grad = (cot_rows[at].astype(f32) * slope).astype(bf16).astype(f32)
            even = jnp.where(inside, grad[:, 0:LANES], 0.0)
            odd = jnp.where(inside, grad[:, LANES:], 0.0)
            g_send[p, slot, :, 0:LANES] = (even + odd).astype(bf16)
            g_send[p, slot, :, LANES : 2 * LANES] = (even + shift(odd, 1, 1)).astype(bf16)

    @pl.when(t != far)
    def _():
        for d in order:
            fine_copy(2, d, p2_send, p2_recv, t, early).wait_recv()
        pl.loop(0, 3)(fine_slot)
        for d in order:
            fine_copy(4, d, g_send, g_recv, lax.rem(lax.rem(t + d, GROUPS), 2), early).start()
        for d in order:
            fine_copy(3, d, p2_send, p2_recv, t, late).wait_recv()

    @pl.when(t == far)
    def _():
        for d in order:
            fine_copy(3, d, p2_send, p2_recv, t, whole).wait_recv()
        pl.loop(0, 3)(fine_slot)

    fine_slot(3)
    fine_grads(1, begun, False)
    g_recv[t] = g_send[core]
    for side in (0, 1):
        halo(side).wait_send()
    for d in range(1, RING):
        near(d).wait_send()
    for m in range(7):
        first(m).wait_send()
    for w in (0, 1):
        for side in (0, 1):
            for n in range(4):
                for hop in (1, 2, 3, 4):
                    if hop < 4 or side == last_side(n):
                        second(w, side, hop, n).wait_send()
        swap_sent(w)
    pair(0, pooled_own, pooled_other).wait_send()
    pair(1, c_own, c_other).wait_send()
    for c in (0, 1):
        for d in order:
            scatter(0, c, p1_send, p1_recv, d).wait_send()
    back = iota((2 * LANES, FINE), 1)
    unpick = jnp.where(
        iota((2 * LANES, FINE), 0) == lax.rem(back, 2) * LANES + lax.div(back, 2) + EDGE, 1.0, 0.0
    ).astype(bf16)
    kept = dot_first(spread, flat(merged_rows[...])).astype(bf16)
    out_ref[0] = dot(kept, unpick).astype(bf16)

    fine_grads(0, arrived, True)
    fine_grads(1, arrived, True)
    columns = [lax.div(column(core, slot), 2) for slot in range(4)]
    block = jnp.concatenate([flat(g_recv[:, slot]) for slot in range(4)], axis=0)

    def back_fine(other, use):
        use = jnp.concatenate(use, axis=0)
        y1[other] = dot_first(block[:, 0:LANES], use[:, 0:640])
        y2[other] = dot_first(block[:, LANES:], use[:, 640:1024])

    back_fine(1, [flat(w2_swap[n]) for n in columns])

    def coarse_part(other):
        total = shift(y1[other, :, 0:192] + y2[other, :, 0:192], -1, 0)
        total = total + y1[other, :, 192:384] + y2[other, :, 192:384]
        total = total + shift(y1[other, :, 384:576], 1, 0)
        return transposed(total, COARSE_C)

    gc_out[...] = coarse_part(1)
    pair(2, gc_out, gc_in).start()
    own_taps(1, columns, lambda use: back_fine(0, use))
    own = coarse_part(0)
    pair(2, gc_out, gc_in).wait_recv()
    grad_c = jnp.where(inside, (own + gc_in[...]) * slope_c[...], 0.0).reshape(4, 2, ROWS, LANES).astype(bf16)
    gc_send[0] = grad_c[:, 0]
    gc_send[1] = grad_c[:, 1]
    for c in (0, 1):
        for d in order:
            gather(6, c, gc_send, gc_recv, d).start()
    gc_recv[t] = gc_send[core]
    pair(2, gc_out, gc_in).wait_send()
    for last in (0, 1):
        fine_sums(last, left)
        fine_grads(last, left, False)
    coarse_row = iota((LANES, FINE), 0)
    widen = jnp.where(coarse_row == lax.div(iota((LANES, FINE), 1), 2) + EDGE, 1.0, 0.0).astype(bf16)
    for c in (0, 1):
        for d in order:
            gather(6, c, gc_send, gc_recv, d).wait_recv()

        coarse_block = jnp.concatenate([flat(gc_recv[:, 2 * c + n]) for n in (0, 1)], axis=0)
        pair_of = [2 * c, 2 * c + 1]

        def back_coarse(other, use, c=c, coarse_block=coarse_block):
            part = dot_first(coarse_block, jnp.concatenate(use, axis=0))
            if c == 0:
                y4[other] = part
            else:
                y4[other] += part

        back_coarse(1, [flat(w1_swap[n]) for n in pair_of])
        if c == 0:
            own_taps(0, pair_of, lambda use: back_coarse(0, use))

    def fine_part(other):
        total = None
        for k in range(5):
            term = shift(y4[other, :, k * FINE_C : (k + 1) * FINE_C], k - 2, 0)
            total = term if total is None else total + term
        return transposed(total, FINE_C)

    gp_out[...] = fine_part(1)
    pair(3, gp_out, gp_in).start()
    own_taps(0, pair_of, lambda use: back_coarse(0, use))
    own = fine_part(0)
    for c in (0, 1):
        for d in order:
            gather(6, c, gc_send, gc_recv, d).wait_send()
    pair(3, gp_out, gp_in).wait_recv()
    total = (own + gp_in[...]) * 0.5
    high = total.astype(bf16)
    low = (total - high.astype(f32)).astype(bf16)
    out_ref[1] = (cot_wide[:, 128 : 128 + FINE].astype(f32) + dot(high, widen) + dot(low, widen)).astype(bf16)

    pair(3, gp_out, gp_in).wait_send()


def shards(enc, w_down, w_up, cot):
    dma = pltpu.SemaphoreType.DMA
    vmem = pltpu.VMEM
    both = pl.pallas_call(
        kernel,
        out_shape=jax.ShapeDtypeStruct((2, FINE_C, FINE), bf16),
        in_specs=[pl.BlockSpec(memory_space=pltpu.HBM)] * 4,
        out_specs=pl.BlockSpec(memory_space=vmem),
        scratch_shapes=[
            vmem((5, OUT1, FINE_C), bf16),
            vmem((5, OUT2, COARSE_C), bf16),
            vmem((2, FINE_C, 128), bf16),
            vmem((2, FINE_C, 128), bf16),
            vmem((FINE_C, WIDE), bf16),
            vmem((FINE_C, WIDE), bf16),
            vmem((RING, 4, 2, ROWS, L1), bf16),
            vmem((4, 4, 2, ROWS, L1), bf16),
            vmem((RING, 4, 2, ROWS, L2), bf16),
            vmem((4, 4, 2, ROWS, L2), bf16),
            vmem((FINE_C, LANES), bf16),
            vmem((FINE_C, LANES), bf16),
            vmem((2 * L1, LANES), bf16),
            vmem((GROUPS, 4, ROWS, LANES), bf16),
            vmem((GROUPS, 4, ROWS, LANES), bf16),
            vmem((COARSE_C, LANES), f32),
            vmem((COARSE_C, LANES), f32),
            vmem((COARSE_C, LANES), bf16),
            vmem((COARSE_C, LANES), bf16),
            vmem((2 * L2, 2 * LANES), bf16),
            vmem((RING, ROWS, 2 * LANES), bf16),
            vmem((RING, ROWS, 2 * LANES), bf16),
            vmem((RING, ROWS, 2 * LANES), bf16),
            vmem((GROUPS, 4, ROWS, 2 * LANES), bf16),
            vmem((GROUPS, 4, ROWS, 2 * LANES), bf16),
            vmem((2, 4, ROWS, 2 * LANES), bf16),
            vmem((GROUPS, 4, ROWS, 2 * LANES), bf16),
            vmem((2, LANES, 640), f32),
            vmem((2, LANES, 384), f32),
            vmem((COARSE_C, LANES), f32),
            vmem((COARSE_C, LANES), f32),
            vmem((2, 4, ROWS, LANES), bf16),
            vmem((GROUPS, 4, ROWS, LANES), bf16),
            vmem((2, LANES, L1), f32),
            vmem((FINE_C, LANES), f32),
            vmem((FINE_C, LANES), f32),
            dma((4,)),
            dma((2,)),
            dma((2,)),
            dma((RING,)),
            dma((RING,)),
            dma((7,)),
            dma((7,)),
            dma((2, 2, 5, 4)),
            dma((2, 2, 5, 4)),
            dma((2, RING)),
            dma((2, RING)),
            dma((4,)),
            dma((4,)),
            dma((8, GROUPS)),
            dma((8, GROUPS)),
        ],
        compiler_params=pltpu.CompilerParams(
            collective_id=0, has_side_effects=True, vmem_limit_bytes=VMEM_LIMIT
        ),
    )(enc[0], cot[0], jnp.swapaxes(w_down, 1, 2), jnp.swapaxes(w_up, 1, 2))
    return both[0:1], both[1:2]


def solution(mesh):
    placed = P(None, "tp", "ctx")
    return jax.shard_map(
        shards,
        mesh=mesh,
        in_specs=(placed,) * 4,
        out_specs=(placed, placed),
        check_vma=False,
    )
```

```python
import jax
import jax.numpy as jnp
from jax import lax
from jax.experimental import pallas as pl
from jax.experimental.pallas import tpu as pltpu
from jax.sharding import PartitionSpec as P

MESH = pl.DeviceIdType.MESH
bf16 = jnp.bfloat16
f32 = jnp.float32
root_half = 0.7071067811865476
norm_scale = 0.3989422804014327

RING = 8
GROUPS = 8
FINE_C, COARSE_C = 176, 192
OUT1, OUT2 = 24, 22
ROWS = 24
L1, L2 = 896, 1024
POS, LANES, EDGE = 192, 256, 32
FINE = 384
WIDE = 128 + FINE + 128
VMEM_LIMIT = 56 << 20


def erf(value):
    return lax.erf(value)


def gelu_value(value):
    return 0.5 * value * (1.0 + erf(value * root_half))


def gelu_both(value):
    cumulative = 0.5 * (1.0 + erf(value * root_half))
    return value * cumulative, cumulative + value * jnp.exp(-0.5 * value * value) * norm_scale


def gelu_slope(value):
    return gelu_both(value)[1]


def dot(a, b):
    return jnp.dot(a, b, preferred_element_type=f32)


def dot_first(a, b):
    return lax.dot_general(a, b, (((0,), (0,)), ((), ())), preferred_element_type=f32)


def iota(shape, dim):
    return lax.broadcasted_iota(jnp.int32, shape, dim)


def flat(block):
    lanes = block.shape[-1]
    return block.reshape(RING * ROWS, lanes)


def transposed(value, width):
    if width < LANES:
        value = jnp.concatenate([value, jnp.zeros((LANES, LANES - width), f32)], axis=1)
    return jnp.transpose(value)[:width]


def shift(value, amount, axis):
    size = value.shape[axis]
    return value if amount % size == 0 else pltpu.roll(value, amount % size, axis=axis)


def kernel(
    enc_in, cot_in, w1_in, w2_in, out_ref, w1_ref, w2_ref,
    edge_out, edge_in, enc_wide, cot_wide, w1_all, w1_swap, w2_all, w2_swap,
    pooled_own, pooled_other, x1, p1_send, p1_recv, pre_c, slope_c, c_own, c_other, x2,
    enc_rows, cot_rows, merged_rows, p2_send, p2_recv, g_send, g_recv, y1, y2, gc_out, gc_in,
    gc_send, gc_recv, y4, gp_out, gp_in,
    in_s, halo_s, halo_r, near_s, near_r, first_s, first_r, second_s, second_r, swap_s, swap_r,
    pair_s, pair_r, tp_s, tp_r,
):
    own = slice(128, 128 + FINE)
    loads = [
        pltpu.make_async_copy(src, dst, in_s.at[n])
        for n, (src, dst) in enumerate(
            ((w1_in, w1_ref), (w2_in, w2_ref), (enc_in, enc_wide.at[:, own]), (cot_in, cot_wide.at[:, own]))
        )
    ]
    for load in loads:
        load.start()
    ctx, t = lax.axis_index("ctx"), lax.axis_index("tp")
    core = lax.rem(t, 2)
    mate = t + 1 - 2 * core
    z, y = lax.div(ctx, RING), lax.rem(ctx, RING)
    one = z + (y - z) * core
    two = y + (z - y) * core

    def ring(index, step):
        return lax.rem(index + RING + step, RING)

    def place(i, j):
        straight, crossed = i * RING + j, j * RING + i
        return straight + (crossed - straight) * core

    def remote(src, dst, send, recv, device):
        return pltpu.make_async_remote_copy(
            src_ref=src, dst_ref=dst, send_sem=send, recv_sem=recv, device_id=device, device_id_type=MESH
        )

    second_to = ((place(one, ring(two, 1)), t), (place(one, ring(two, -1)), t))
    count = RING * RING
    ctx_next, ctx_prev = lax.rem(ctx + 1, count), lax.rem(ctx + count - 1, count)

    barrier = pltpu.get_barrier_semaphore()
    partners = [(place(ring(one, d), two), t) for d in range(1, RING)]
    partners += [*second_to, (ctx_next, t), (ctx_prev, t)]
    partners += [(ctx, lax.rem(t + d, GROUPS)) for d in range(1, GROUPS)]
    for device in partners:
        pl.semaphore_signal(barrier, inc=1, device_id=device, device_id_type=MESH)

    for load in loads:
        load.wait()
    taps = ((w1_all, w1_swap), (w2_all, w2_swap))
    down = [w1_ref[k].astype(f32) for k in range(5)]
    up = [w2_ref[k].astype(f32) for k in range(5)]
    down = jnp.concatenate([*down, jnp.zeros((OUT1, 16), f32)], axis=1)
    up = jnp.concatenate([up[0], up[2], up[4], jnp.zeros((OUT2, 64), f32), up[1], up[3]], axis=1)
    up = jnp.concatenate([up, jnp.zeros((ROWS - OUT2, L2), f32)], axis=0)
    for w_all, block in ((w1_all, down), (w2_all, up)):
        w_all[two, lax.div(one, 2), lax.rem(one, 2)] = block.astype(bf16)
    low = iota((FINE_C, 128), 1) < 64
    last, first_tile = slice(FINE, 128 + FINE), slice(128, 256)
    enc_last, cot_last = enc_wide[:, last].astype(f32), shift(cot_wide[:, last].astype(f32), 64, 1)
    enc_first, cot_first = enc_wide[:, first_tile].astype(f32), shift(cot_wide[:, first_tile].astype(f32), 64, 1)
    edge_out[0] = jnp.where(low, cot_last, enc_last).astype(bf16)
    edge_out[1] = jnp.where(low, enc_first, cot_first).astype(bf16)
    pl.semaphore_wait(barrier, len(partners))

    def halo(side):
        to = ctx_next if side == 0 else ctx_prev
        return remote(edge_out.at[side], edge_in.at[side], halo_s.at[side], halo_r.at[side], (to, t))

    def near(d):
        block = w1_all.at[two, lax.div(one, 2), lax.rem(one, 2)]
        return remote(block, block, near_s.at[d], near_r.at[d], (place(ring(one, d), two), t))

    def near_arrives(j):
        d = ring(one, -j)
        block = w1_all.at[two, lax.div(j, 2), lax.rem(j, 2)]
        remote(block, block, near_s.at[d], near_r.at[d], (place(ring(one, d), two), t)).wait_recv()

    sign = 1 - 2 * lax.rem(one, 2)
    routes = ((0, 1), (0, -1), (0, 2), (0, -2), (-2, 1), (-2 * sign, 2 * sign), (2, -1))

    def first(m, arriving=False):
        origin, step = routes[m]
        index = ring(one, origin - step if arriving else origin)
        block = w2_all.at[two, lax.div(index, 2), lax.rem(index, 2)]
        return remote(block, block, first_s.at[m], first_r.at[m], (place(ring(one, step), two), t))

    def piece(n):
        return lax.rem(lax.div(one, 2) + (0, 1, 3, 2)[n], 4)

    def second(w, side, hop, n, arriving=False):
        step = hop if arriving else hop - 1
        index = ring(two, -step if side == 0 else step)
        block = taps[w][0].at[index, piece(n)]
        return remote(block, block, second_s.at[w, side, hop, n], second_r.at[w, side, hop, n], second_to[side])

    def swap_zero(w, index):
        return remote(
            taps[w][0].at[index], taps[w][1].at[lax.div(index, 2)],
            swap_s.at[w, lax.div(index, 2)], swap_r.at[w, lax.div(index, 2)], (ctx, mate),
        )

    def swap_one(w, index):
        return remote(
            taps[w][0].at[index, :, 0], taps[w][1].at[:, lax.div(index, 2), lax.rem(index, 2)],
            swap_s.at[w, index], swap_r.at[w, index], (ctx, mate),
        )

    def swap(w, index):
        @pl.when(jnp.logical_and(core == 0, lax.rem(index, 2) == 1))
        def _():
            swap_zero(w, index).start()

        @pl.when(core == 1)
        def _():
            swap_one(w, index).start()

    def swap_done(w):
        @pl.when(core == 0)
        def _():
            for index in range(RING):
                swap_one(w, index).wait_recv()

        @pl.when(core == 1)
        def _():
            for index in range(1, RING, 2):
                swap_zero(w, index).wait_recv()

    def swap_sent(w):
        @pl.when(core == 0)
        def _():
            for index in range(1, RING, 2):
                swap_zero(w, index).wait_send()

        @pl.when(core == 1)
        def _():
            for index in range(RING):
                swap_one(w, index).wait_send()

    def last_side(n):
        return 0 if n < 2 else 1

    def second_start(w, n):
        for side in (0, 1):
            second(w, side, 1, n).start()

    def second_part(w, hop, n):
        for side in (0, 1):
            second(w, side, hop, n, True).wait_recv()
            if hop < 3 or side == last_side(n):
                second(w, side, hop + 1, n).start()

    def second_swap(w, hop):
        swap(w, ring(two, hop))
        swap(w, ring(two, -hop))

    def second_step(w, hop):
        if hop < 4:
            for n in range(4):
                second_part(w, hop, n)
            second_swap(w, hop)
        else:
            for n in range(4):
                second(w, last_side(n), 4, n, True).wait_recv()
            swap(w, ring(two, 4))

    def pair(n, src, dst):
        return remote(src, dst, pair_s.at[n], pair_r.at[n], (ctx, mate))

    def to_group(n, d, src, dst):
        return remote(src, dst, tp_s.at[n, d], tp_r.at[n, d], (ctx, lax.rem(t + d, GROUPS)))

    def scatter(n, c, send, recv, d):
        part = pl.ds(2 * c, 2)
        return to_group(n + c, d, send.at[lax.rem(t + d, GROUPS), part], recv.at[t, part])

    def gather(n, c, send, recv, d):
        part = pl.ds(2 * c, 2)
        return to_group(n + c, d, send.at[lax.rem(lax.rem(t + d, GROUPS), 2), part], recv.at[t, part])

    order = (4, 3, 5, 2, 6, 1, 7)

    far = ring(z, 4)
    rows_near = [ring(z, k) for k in range(-3, 4)]

    def column(parity, slot):
        return lax.rem(y + RING - 2 - lax.rem(y + parity, 2) + 2 * slot, RING)

    def conv_fine(blocks):
        mine, swapped = [], []
        for slot, i in blocks:
            q, upper, lower = lax.div(column(core, slot), 2), lax.div(i, 2), lax.rem(i, 2)
            at = (2 * q + (i - 2 * q) * core, upper + (q - upper) * core, lower + (1 - lower) * core)
            mine.append(w2_all[at].astype(f32))
            swapped.append(w2_swap[q, upper, lower].astype(f32))
        mine, swapped = (jnp.concatenate(part, axis=0).astype(bf16) for part in (mine, swapped))
        sums = dot(mine, x2[0:L2]) + dot(swapped, x2[L2 : 2 * L2])
        for n, (slot, i) in enumerate(blocks):
            p2_send[i, slot] = sums[n * ROWS : (n + 1) * ROWS].astype(bf16)

    def fine_swap_done(last):
        @pl.when(core == 0)
        def _():
            for i in (far,) if last else rows_near:
                swap_one(1, i).wait_recv()

        @pl.when(core == 1)
        def _():
            for slot in (3,) if last else (0, 1, 2):
                swap_zero(1, column(1, slot)).wait_recv()

    def fine_copy(n, d, send, recv, index, slots):
        return to_group(n, d, send.at[index, slots], recv.at[t, slots])

    early, late, whole = pl.ds(0, 3), pl.ds(3, 1), pl.ds(0, 4)

    def fine_sums(last, act):
        for d in order:
            target = lax.rem(t + d, GROUPS)

            @pl.when(target != far)
            def _():
                act(fine_copy(2 + last, d, p2_send, p2_recv, target, late if last else early))

            if last:

                @pl.when(target == far)
                def _():
                    act(fine_copy(3, d, p2_send, p2_recv, target, whole))

    def fine_grads(last, act, source):
        for d in order:
            target = lax.rem(t + d, GROUPS)
            origin = ring(t, -d) if source else t

            @pl.when(origin != far)
            def _():
                act(fine_copy(4 + last, d, g_send, g_recv, lax.rem(target, 2), late if last else early))

            if last:

                @pl.when(origin == far)
                def _():
                    act(fine_copy(5, d, g_send, g_recv, lax.rem(target, 2), whole))

    def begun(copy):
        copy.start()

    def arrived(copy):
        copy.wait_recv()

    def left(copy):
        copy.wait_send()

    def own_taps(w, q, use):
        w_all = taps[w][0]

        @pl.when(core == 0)
        def _():
            use([flat(w_all[2 * n]) for n in q])

        @pl.when(core == 1)
        def _():
            use([flat(w_all[:, n, 1]) for n in q])

    for d in (1, 7, 2, 6, 3, 5, 4):
        near(d).start()
    near_arrives(one + 1 - 2 * lax.rem(one, 2))
    second_start(0, 0)
    for n in (1, 2, 3):
        near_arrives(2 * piece(n))
        near_arrives(2 * piece(n) + 1)
        second_start(0, n)
    swap(0, two)
    for m in range(4):
        first(m).start()
    for side in (0, 1):
        halo(side).start()

    lane = iota((WIDE, 2 * LANES), 1)
    row = iota((WIDE, 2 * LANES), 0)
    half_lane = lax.rem(lane, LANES)
    pick = jnp.where(row == 2 * half_lane + 64 + lax.div(lane, LANES), 1.0, 0.0).astype(bf16)
    where_to = iota((RING * ROWS, FINE_C), 1)
    spread = jnp.where(
        iota((RING * ROWS, FINE_C), 0) == lax.div(where_to, OUT2) * ROWS + lax.rem(where_to, OUT2), 1.0, 0.0
    ).astype(bf16)
    at = ctx * POS + iota((1, LANES), 1) - EDGE
    inside = jnp.logical_and(at >= 0, at < count * POS)
    second_step(0, 1)
    for m in (2, 3):
        first(m, True).wait_recv()
    for m in (4, 5, 6):
        first(m).start()
    for side in (0, 1):
        halo(side).wait_recv()
        lanes = slice(0, 128) if side == 0 else slice(128 + FINE, WIDE)
        enc_wide[:, lanes] = edge_in[side]
        cot_wide[:, lanes] = shift(edge_in[side].astype(f32), 64, 1).astype(bf16)
    enc_ed = dot(enc_wide[...], pick)
    pooled = jnp.where(inside, (enc_ed[:, 0:LANES] + enc_ed[:, LANES:]) * 0.5, 0.0)
    pooled_own[...] = pooled.astype(bf16)
    pair(0, pooled_own, pooled_other).start()
    second_step(0, 2)
    for m in (0, 1, 4, 5, 6):
        first(m, True).wait_recv()
    for n in range(4):
        second_start(1, n)
    swap(1, two)
    enc_rows[...] = dot(spread, enc_ed.astype(bf16)).reshape(RING, ROWS, 2 * LANES).astype(bf16)
    cot_ed = dot(cot_wide[...], pick).astype(bf16)
    cot_rows[...] = dot(spread, cot_ed).reshape(RING, ROWS, 2 * LANES).astype(bf16)
    pair(0, pooled_own, pooled_other).wait_recv()
    for other, ref in enumerate((pooled_own, pooled_other)):
        value = ref[...].astype(f32)
        for k in range(5):
            start = other * L1 + k * FINE_C
            x1[start : start + FINE_C] = shift(value, 2 - k, 1).astype(bf16)
        x1[other * L1 + 880 : (other + 1) * L1] = jnp.zeros((16, LANES), bf16)
    second_step(0, 3)
    for n in range(4):
        second_part(1, 1, n)
    second_swap(1, 1)
    second_step(0, 4)
    second_step(1, 2)

    for c in (0, 1):
        if c == 0:
            swap_done(0)

        @pl.loop(2 * c, 2 * c + 2)
        def _(q):
            swapped = dot(flat(w1_swap[q]), x1[L1 : 2 * L1])

            def use(mine):
                part = dot(mine[0], x1[0:L1]) + swapped
                p1_send[:, q] = part.reshape(RING, ROWS, LANES).astype(bf16)

            own_taps(0, [q], use)

        for d in order:
            scatter(0, c, p1_send, p1_recv, d).start()

    p1_recv[t] = p1_send[t]
    second_step(1, 3)
    for c in (0, 1):
        for d in order:
            scatter(0, c, p1_send, p1_recv, d).wait_recv()
    sides = [sum(p1_recv[2 * x + p].astype(f32) for x in range(4)) for p in (0, 1)]
    pre_c[...] = jnp.stack(sides, axis=1).reshape(COARSE_C, LANES)
    c_own[...] = jnp.where(inside, gelu_value(pre_c[...]), 0.0).astype(bf16)
    pair(1, c_own, c_other).start()
    slope_c[...] = gelu_slope(pre_c[...])
    pair(1, c_own, c_other).wait_recv()
    for other, ref in enumerate((c_own, c_other)):
        value = ref[...]
        wide = value.astype(f32)
        before, after = shift(wide, 1, 1).astype(bf16), shift(wide, -1, 1).astype(bf16)
        for start, even, odd in (
            (0, before, before),
            (192, value, value),
            (384, after, after),
            (640, before, value),
            (832, value, after),
        ):
            start += other * L2
            x2[start : start + COARSE_C, 0:LANES] = even
            x2[start : start + COARSE_C, LANES : 2 * LANES] = odd
        x2[other * L2 + 576 : other * L2 + 640] = jnp.zeros((64, 2 * LANES), bf16)
    fine_swap_done(0)
    conv_fine([(slot, i) for slot in range(3) for i in rows_near])
    fine_sums(0, begun)
    second_step(1, 4)
    fine_swap_done(1)
    conv_fine([(slot, far) for slot in range(4)] + [(3, i) for i in rows_near])
    fine_sums(1, begun)
    p2_recv[t] = p2_send[t]

    def fine_slot(slot):
        for p in (0, 1):
            pre = sum(p2_recv[2 * x + p, slot].astype(f32) for x in range(4))
            value, slope = gelu_both(pre)
            at = column(p, slot)
            merged_rows[at] = (enc_rows[at].astype(f32) + value).astype(bf16)
            grad = (cot_rows[at].astype(f32) * slope).astype(bf16).astype(f32)
            even = jnp.where(inside, grad[:, 0:LANES], 0.0)
            odd = jnp.where(inside, grad[:, LANES:], 0.0)
            g_send[p, slot, :, 0:LANES] = (even + odd).astype(bf16)
            g_send[p, slot, :, LANES : 2 * LANES] = (even + shift(odd, 1, 1)).astype(bf16)

    @pl.when(t != far)
    def _():
        for d in order:
            fine_copy(2, d, p2_send, p2_recv, t, early).wait_recv()
        pl.loop(0, 3)(fine_slot)
        for d in order:
            fine_copy(4, d, g_send, g_recv, lax.rem(lax.rem(t + d, GROUPS), 2), early).start()
        for d in order:
            fine_copy(3, d, p2_send, p2_recv, t, late).wait_recv()

    @pl.when(t == far)
    def _():
        for d in order:
            fine_copy(3, d, p2_send, p2_recv, t, whole).wait_recv()
        pl.loop(0, 3)(fine_slot)

    fine_slot(3)
    fine_grads(1, begun, False)
    g_recv[t] = g_send[core]
    for side in (0, 1):
        halo(side).wait_send()
    for d in range(1, RING):
        near(d).wait_send()
    for m in range(7):
        first(m).wait_send()
    for w in (0, 1):
        for side in (0, 1):
            for n in range(4):
                for hop in (1, 2, 3, 4):
                    if hop < 4 or side == last_side(n):
                        second(w, side, hop, n).wait_send()
        swap_sent(w)
    pair(0, pooled_own, pooled_other).wait_send()
    pair(1, c_own, c_other).wait_send()
    for c in (0, 1):
        for d in order:
            scatter(0, c, p1_send, p1_recv, d).wait_send()
    back = iota((2 * LANES, FINE), 1)
    unpick = jnp.where(
        iota((2 * LANES, FINE), 0) == lax.rem(back, 2) * LANES + lax.div(back, 2) + EDGE, 1.0, 0.0
    ).astype(bf16)
    kept = dot_first(spread, flat(merged_rows[...])).astype(bf16)
    out_ref[0] = dot(kept, unpick).astype(bf16)

    fine_grads(0, arrived, True)
    fine_grads(1, arrived, True)
    columns = [lax.div(column(core, slot), 2) for slot in range(4)]
    block = jnp.concatenate([flat(g_recv[:, slot]) for slot in range(4)], axis=0)

    def back_fine(other, use):
        use = jnp.concatenate(use, axis=0)
        y1[other] = dot_first(block[:, 0:LANES], use[:, 0:640])
        y2[other] = dot_first(block[:, LANES:], use[:, 640:1024])

    back_fine(1, [flat(w2_swap[n]) for n in columns])

    def coarse_part(other):
        total = shift(y1[other, :, 0:192] + y2[other, :, 0:192], -1, 0)
        total = total + y1[other, :, 192:384] + y2[other, :, 192:384]
        total = total + shift(y1[other, :, 384:576], 1, 0)
        return transposed(total, COARSE_C)

    gc_out[...] = coarse_part(1)
    pair(2, gc_out, gc_in).start()
    own_taps(1, columns, lambda use: back_fine(0, use))
    own = coarse_part(0)
    pair(2, gc_out, gc_in).wait_recv()
    grad_c = jnp.where(inside, (own + gc_in[...]) * slope_c[...], 0.0).reshape(4, 2, ROWS, LANES).astype(bf16)
    gc_send[0] = grad_c[:, 0]
    gc_send[1] = grad_c[:, 1]
    for c in (0, 1):
        for d in order:
            gather(6, c, gc_send, gc_recv, d).start()
    gc_recv[t] = gc_send[core]
    pair(2, gc_out, gc_in).wait_send()
    for last in (0, 1):
        fine_sums(last, left)
        fine_grads(last, left, False)
    coarse_row = iota((LANES, FINE), 0)
    widen = jnp.where(coarse_row == lax.div(iota((LANES, FINE), 1), 2) + EDGE, 1.0, 0.0).astype(bf16)
    for c in (0, 1):
        for d in order:
            gather(6, c, gc_send, gc_recv, d).wait_recv()

        coarse_block = jnp.concatenate([flat(gc_recv[:, 2 * c + n]) for n in (0, 1)], axis=0)
        pair_of = [2 * c, 2 * c + 1]

        def back_coarse(other, use, c=c, coarse_block=coarse_block):
            part = dot_first(coarse_block, jnp.concatenate(use, axis=0))
            if c == 0:
                y4[other] = part
            else:
                y4[other] += part

        back_coarse(1, [flat(w1_swap[n]) for n in pair_of])
        if c == 0:
            own_taps(0, pair_of, lambda use: back_coarse(0, use))

    def fine_part(other):
        total = None
        for k in range(5):
            term = shift(y4[other, :, k * FINE_C : (k + 1) * FINE_C], k - 2, 0)
            total = term if total is None else total + term
        return transposed(total, FINE_C)

    gp_out[...] = fine_part(1)
    pair(3, gp_out, gp_in).start()
    own_taps(0, pair_of, lambda use: back_coarse(0, use))
    own = fine_part(0)
    for c in (0, 1):
        for d in order:
            gather(6, c, gc_send, gc_recv, d).wait_send()
    pair(3, gp_out, gp_in).wait_recv()
    total = (own + gp_in[...]) * 0.5
    high = total.astype(bf16)
    low = (total - high.astype(f32)).astype(bf16)
    out_ref[1] = (cot_wide[:, 128 : 128 + FINE].astype(f32) + dot(high, widen) + dot(low, widen)).astype(bf16)

    pair(3, gp_out, gp_in).wait_send()


def shards(enc, w_down, w_up, cot):
    dma = pltpu.SemaphoreType.DMA
    vmem = pltpu.VMEM
    both = pl.pallas_call(
        kernel,
        out_shape=jax.ShapeDtypeStruct((2, FINE_C, FINE), bf16),
        in_specs=[pl.BlockSpec(memory_space=pltpu.HBM)] * 4,
        out_specs=pl.BlockSpec(memory_space=vmem),
        scratch_shapes=[
            vmem((5, OUT1, FINE_C), bf16),
            vmem((5, OUT2, COARSE_C), bf16),
            vmem((2, FINE_C, 128), bf16),
            vmem((2, FINE_C, 128), bf16),
            vmem((FINE_C, WIDE), bf16),
            vmem((FINE_C, WIDE), bf16),
            vmem((RING, 4, 2, ROWS, L1), bf16),
            vmem((4, 4, 2, ROWS, L1), bf16),
            vmem((RING, 4, 2, ROWS, L2), bf16),
            vmem((4, 4, 2, ROWS, L2), bf16),
            vmem((FINE_C, LANES), bf16),
            vmem((FINE_C, LANES), bf16),
            vmem((2 * L1, LANES), bf16),
            vmem((GROUPS, 4, ROWS, LANES), bf16),
            vmem((GROUPS, 4, ROWS, LANES), bf16),
            vmem((COARSE_C, LANES), f32),
            vmem((COARSE_C, LANES), f32),
            vmem((COARSE_C, LANES), bf16),
            vmem((COARSE_C, LANES), bf16),
            vmem((2 * L2, 2 * LANES), bf16),
            vmem((RING, ROWS, 2 * LANES), bf16),
            vmem((RING, ROWS, 2 * LANES), bf16),
            vmem((RING, ROWS, 2 * LANES), bf16),
            vmem((GROUPS, 4, ROWS, 2 * LANES), bf16),
            vmem((GROUPS, 4, ROWS, 2 * LANES), bf16),
            vmem((2, 4, ROWS, 2 * LANES), bf16),
            vmem((GROUPS, 4, ROWS, 2 * LANES), bf16),
            vmem((2, LANES, 640), f32),
            vmem((2, LANES, 384), f32),
            vmem((COARSE_C, LANES), f32),
            vmem((COARSE_C, LANES), f32),
            vmem((2, 4, ROWS, LANES), bf16),
            vmem((GROUPS, 4, ROWS, LANES), bf16),
            vmem((2, LANES, L1), f32),
            vmem((FINE_C, LANES), f32),
            vmem((FINE_C, LANES), f32),
            dma((4,)),
            dma((2,)),
            dma((2,)),
            dma((RING,)),
            dma((RING,)),
            dma((7,)),
            dma((7,)),
            dma((2, 2, 5, 4)),
            dma((2, 2, 5, 4)),
            dma((2, RING)),
            dma((2, RING)),
            dma((4,)),
            dma((4,)),
            dma((8, GROUPS)),
            dma((8, GROUPS)),
        ],
        compiler_params=pltpu.CompilerParams(
            collective_id=0, has_side_effects=True, vmem_limit_bytes=VMEM_LIMIT
        ),
    )(enc[0], cot[0], jnp.swapaxes(w_down, 1, 2), jnp.swapaxes(w_up, 1, 2))
    return both[0:1], both[1:2]


def solution(mesh):
    placed = P(None, "tp", "ctx")
    return jax.shard_map(
        shards,
        mesh=mesh,
        in_specs=(placed,) * 4,
        out_specs=(placed, placed),
        check_vma=False,
    )
```

```python
import jax
import jax.numpy as jnp
from jax import lax
from jax.experimental import pallas as pl
from jax.experimental.pallas import tpu as pltpu
from jax.sharding import PartitionSpec as P

MESH = pl.DeviceIdType.MESH
bf16 = jnp.bfloat16
f32 = jnp.float32
root_half = 0.7071067811865476
norm_scale = 0.3989422804014327

RING = 8
GROUPS = 8
FINE_C, COARSE_C = 176, 192
OUT1, OUT2 = 24, 22
ROWS = 24
L1, L2 = 896, 1024
POS, LANES, EDGE = 192, 256, 32
FINE = 384
WIDE = 128 + FINE + 128
VMEM_LIMIT = 56 << 20


def erf(value):
    return lax.erf(value)


def gelu_value(value):
    return 0.5 * value * (1.0 + erf(value * root_half))


def gelu_both(value):
    cumulative = 0.5 * (1.0 + erf(value * root_half))
    return value * cumulative, cumulative + value * jnp.exp(-0.5 * value * value) * norm_scale


def gelu_slope(value):
    return gelu_both(value)[1]


def dot(a, b):
    return jnp.dot(a, b, preferred_element_type=f32)


def dot_first(a, b):
    return lax.dot_general(a, b, (((0,), (0,)), ((), ())), preferred_element_type=f32)


def iota(shape, dim):
    return lax.broadcasted_iota(jnp.int32, shape, dim)


def flat(block):
    lanes = block.shape[-1]
    return block.reshape(RING * ROWS, lanes)


def transposed(value, width):
    if width < LANES:
        value = jnp.concatenate([value, jnp.zeros((LANES, LANES - width), f32)], axis=1)
    return jnp.transpose(value)[:width]


def shift(value, amount, axis):
    size = value.shape[axis]
    return value if amount % size == 0 else pltpu.roll(value, amount % size, axis=axis)


def kernel(
    enc_in, cot_in, w1_in, w2_in, out_ref, w1_ref, w2_ref,
    edge_out, edge_in, enc_wide, cot_wide, w1_all, w1_swap, w2_all, w2_swap,
    pooled_own, pooled_other, x1, p1_send, p1_recv, pre_c, slope_c, c_own, c_other, x2,
    enc_rows, cot_rows, merged_rows, p2_send, p2_recv, g_send, g_recv, y1, y2, gc_out, gc_in,
    gc_send, gc_recv, y4, gp_out, gp_in,
    in_s, halo_s, halo_r, near_s, near_r, first_s, first_r, second_s, second_r, swap_s, swap_r,
    pair_s, pair_r, tp_s, tp_r,
):
    own = slice(128, 128 + FINE)
    loads = [
        pltpu.make_async_copy(src, dst, in_s.at[n])
        for n, (src, dst) in enumerate(
            ((w1_in, w1_ref), (w2_in, w2_ref), (enc_in, enc_wide.at[:, own]), (cot_in, cot_wide.at[:, own]))
        )
    ]
    for load in loads:
        load.start()
    ctx, t = lax.axis_index("ctx"), lax.axis_index("tp")
    core = lax.rem(t, 2)
    mate = t + 1 - 2 * core
    z, y = lax.div(ctx, RING), lax.rem(ctx, RING)
    one = z + (y - z) * core
    two = y + (z - y) * core

    def ring(index, step):
        return lax.rem(index + RING + step, RING)

    def place(i, j):
        straight, crossed = i * RING + j, j * RING + i
        return straight + (crossed - straight) * core

    def remote(src, dst, send, recv, device):
        return pltpu.make_async_remote_copy(
            src_ref=src, dst_ref=dst, send_sem=send, recv_sem=recv, device_id=device, device_id_type=MESH
        )

    second_to = ((place(one, ring(two, 1)), t), (place(one, ring(two, -1)), t))
    count = RING * RING
    ctx_next, ctx_prev = lax.rem(ctx + 1, count), lax.rem(ctx + count - 1, count)

    barrier = pltpu.get_barrier_semaphore()
    partners = [(place(ring(one, d), two), t) for d in range(1, RING)]
    partners += [*second_to, (ctx_next, t), (ctx_prev, t)]
    partners += [(ctx, lax.rem(t + d, GROUPS)) for d in range(1, GROUPS)]
    for device in partners:
        pl.semaphore_signal(barrier, inc=1, device_id=device, device_id_type=MESH)

    for load in loads:
        load.wait()
    taps = ((w1_all, w1_swap), (w2_all, w2_swap))
    down = [w1_ref[k].astype(f32) for k in range(5)]
    up = [w2_ref[k].astype(f32) for k in range(5)]
    down = jnp.concatenate([*down, jnp.zeros((OUT1, 16), f32)], axis=1)
    up = jnp.concatenate([up[0], up[2], up[4], jnp.zeros((OUT2, 64), f32), up[1], up[3]], axis=1)
    up = jnp.concatenate([up, jnp.zeros((ROWS - OUT2, L2), f32)], axis=0)
    for w_all, block in ((w1_all, down), (w2_all, up)):
        w_all[two, lax.div(one, 2), lax.rem(one, 2)] = block.astype(bf16)
    low = iota((FINE_C, 128), 1) < 64
    last, first_tile = slice(FINE, 128 + FINE), slice(128, 256)
    enc_last, cot_last = enc_wide[:, last].astype(f32), shift(cot_wide[:, last].astype(f32), 64, 1)
    enc_first, cot_first = enc_wide[:, first_tile].astype(f32), shift(cot_wide[:, first_tile].astype(f32), 64, 1)
    edge_out[0] = jnp.where(low, cot_last, enc_last).astype(bf16)
    edge_out[1] = jnp.where(low, enc_first, cot_first).astype(bf16)
    pl.semaphore_wait(barrier, len(partners))

    def halo(side):
        to = ctx_next if side == 0 else ctx_prev
        return remote(edge_out.at[side], edge_in.at[side], halo_s.at[side], halo_r.at[side], (to, t))

    def near(d):
        block = w1_all.at[two, lax.div(one, 2), lax.rem(one, 2)]
        return remote(block, block, near_s.at[d], near_r.at[d], (place(ring(one, d), two), t))

    def near_arrives(j):
        d = ring(one, -j)
        block = w1_all.at[two, lax.div(j, 2), lax.rem(j, 2)]
        remote(block, block, near_s.at[d], near_r.at[d], (place(ring(one, d), two), t)).wait_recv()

    sign = 1 - 2 * lax.rem(one, 2)
    routes = ((0, 1), (0, -1), (0, 2), (0, -2), (-2, 1), (-2 * sign, 2 * sign), (2, -1))

    def first(m, arriving=False):
        origin, step = routes[m]
        index = ring(one, origin - step if arriving else origin)
        block = w2_all.at[two, lax.div(index, 2), lax.rem(index, 2)]
        return remote(block, block, first_s.at[m], first_r.at[m], (place(ring(one, step), two), t))

    def piece(n):
        return lax.rem(lax.div(one, 2) + (0, 1, 3, 2)[n], 4)

    def second(w, side, hop, n, arriving=False):
        step = hop if arriving else hop - 1
        index = ring(two, -step if side == 0 else step)
        block = taps[w][0].at[index, piece(n)]
        return remote(block, block, second_s.at[w, side, hop, n], second_r.at[w, side, hop, n], second_to[side])

    def swap_zero(w, index):
        return remote(
            taps[w][0].at[index], taps[w][1].at[lax.div(index, 2)],
            swap_s.at[w, lax.div(index, 2)], swap_r.at[w, lax.div(index, 2)], (ctx, mate),
        )

    def swap_one(w, index):
        return remote(
            taps[w][0].at[index, :, 0], taps[w][1].at[:, lax.div(index, 2), lax.rem(index, 2)],
            swap_s.at[w, index], swap_r.at[w, index], (ctx, mate),
        )

    def swap(w, index):
        @pl.when(jnp.logical_and(core == 0, lax.rem(index, 2) == 1))
        def _():
            swap_zero(w, index).start()

        @pl.when(core == 1)
        def _():
            swap_one(w, index).start()

    def swap_done(w):
        @pl.when(core == 0)
        def _():
            for index in range(RING):
                swap_one(w, index).wait_recv()

        @pl.when(core == 1)
        def _():
            for index in range(1, RING, 2):
                swap_zero(w, index).wait_recv()

    def swap_sent(w):
        @pl.when(core == 0)
        def _():
            for index in range(1, RING, 2):
                swap_zero(w, index).wait_send()

        @pl.when(core == 1)
        def _():
            for index in range(RING):
                swap_one(w, index).wait_send()

    def last_side(n):
        return 0 if n < 2 else 1

    def second_start(w, n):
        for side in (0, 1):
            second(w, side, 1, n).start()

    def second_part(w, hop, n):
        for side in (0, 1):
            second(w, side, hop, n, True).wait_recv()
            if hop < 3 or side == last_side(n):
                second(w, side, hop + 1, n).start()

    def second_swap(w, hop):
        swap(w, ring(two, hop))
        swap(w, ring(two, -hop))

    def second_step(w, hop):
        if hop < 4:
            for n in range(4):
                second_part(w, hop, n)
            second_swap(w, hop)
        else:
            for n in range(4):
                second(w, last_side(n), 4, n, True).wait_recv()
            swap(w, ring(two, 4))

    def pair(n, src, dst):
        return remote(src, dst, pair_s.at[n], pair_r.at[n], (ctx, mate))

    def to_group(n, d, src, dst):
        return remote(src, dst, tp_s.at[n, d], tp_r.at[n, d], (ctx, lax.rem(t + d, GROUPS)))

    def scatter(n, c, send, recv, d):
        part = pl.ds(2 * c, 2)
        return to_group(n + c, d, send.at[lax.rem(t + d, GROUPS), part], recv.at[t, part])

    def gather(n, c, send, recv, d):
        part = pl.ds(2 * c, 2)
        return to_group(n + c, d, send.at[lax.rem(lax.rem(t + d, GROUPS), 2), part], recv.at[t, part])

    order = (4, 2, 6, 3, 5, 1, 7)

    far = ring(z, 4)
    rows_near = [ring(z, k) for k in range(-3, 4)]

    def column(parity, slot):
        return lax.rem(y + RING - 2 - lax.rem(y + parity, 2) + 2 * slot, RING)

    def conv_fine(blocks):
        mine, swapped = [], []
        for slot, i in blocks:
            q, upper, lower = lax.div(column(core, slot), 2), lax.div(i, 2), lax.rem(i, 2)
            at = (2 * q + (i - 2 * q) * core, upper + (q - upper) * core, lower + (1 - lower) * core)
            mine.append(w2_all[at].astype(f32))
            swapped.append(w2_swap[q, upper, lower].astype(f32))
        mine, swapped = (jnp.concatenate(part, axis=0).astype(bf16) for part in (mine, swapped))
        sums = dot(mine, x2[0:L2]) + dot(swapped, x2[L2 : 2 * L2])
        for n, (slot, i) in enumerate(blocks):
            p2_send[i, slot] = sums[n * ROWS : (n + 1) * ROWS].astype(bf16)

    def fine_swap_done(last):
        @pl.when(core == 0)
        def _():
            for i in (far,) if last else rows_near:
                swap_one(1, i).wait_recv()

        @pl.when(core == 1)
        def _():
            for slot in (3,) if last else (0, 1, 2):
                swap_zero(1, column(1, slot)).wait_recv()

    def fine_copy(n, d, send, recv, index, slots):
        return to_group(n, d, send.at[index, slots], recv.at[t, slots])

    early, late, whole = pl.ds(0, 3), pl.ds(3, 1), pl.ds(0, 4)

    def fine_sums(last, act):
        for d in order:
            target = lax.rem(t + d, GROUPS)

            @pl.when(target != far)
            def _():
                act(fine_copy(2 + last, d, p2_send, p2_recv, target, late if last else early))

            if last:

                @pl.when(target == far)
                def _():
                    act(fine_copy(3, d, p2_send, p2_recv, target, whole))

    def fine_grads(last, act, source):
        for d in order:
            target = lax.rem(t + d, GROUPS)
            origin = ring(t, -d) if source else t

            @pl.when(origin != far)
            def _():
                act(fine_copy(4 + last, d, g_send, g_recv, lax.rem(target, 2), late if last else early))

            if last:

                @pl.when(origin == far)
                def _():
                    act(fine_copy(5, d, g_send, g_recv, lax.rem(target, 2), whole))

    def begun(copy):
        copy.start()

    def arrived(copy):
        copy.wait_recv()

    def left(copy):
        copy.wait_send()

    def own_taps(w, q, use):
        w_all = taps[w][0]

        @pl.when(core == 0)
        def _():
            use([flat(w_all[2 * n]) for n in q])

        @pl.when(core == 1)
        def _():
            use([flat(w_all[:, n, 1]) for n in q])

    for d in (1, 7, 2, 6, 3, 5, 4):
        near(d).start()
    near_arrives(one + 1 - 2 * lax.rem(one, 2))
    second_start(0, 0)
    for n in (1, 2, 3):
        near_arrives(2 * piece(n))
        near_arrives(2 * piece(n) + 1)
        second_start(0, n)
    swap(0, two)
    for m in range(4):
        first(m).start()
    for side in (0, 1):
        halo(side).start()

    lane = iota((WIDE, 2 * LANES), 1)
    row = iota((WIDE, 2 * LANES), 0)
    half_lane = lax.rem(lane, LANES)
    pick = jnp.where(row == 2 * half_lane + 64 + lax.div(lane, LANES), 1.0, 0.0).astype(bf16)
    where_to = iota((RING * ROWS, FINE_C), 1)
    spread = jnp.where(
        iota((RING * ROWS, FINE_C), 0) == lax.div(where_to, OUT2) * ROWS + lax.rem(where_to, OUT2), 1.0, 0.0
    ).astype(bf16)
    at = ctx * POS + iota((1, LANES), 1) - EDGE
    inside = jnp.logical_and(at >= 0, at < count * POS)
    second_step(0, 1)
    for m in (2, 3):
        first(m, True).wait_recv()
    for m in (4, 5, 6):
        first(m).start()
    for side in (0, 1):
        halo(side).wait_recv()
        lanes = slice(0, 128) if side == 0 else slice(128 + FINE, WIDE)
        enc_wide[:, lanes] = edge_in[side]
        cot_wide[:, lanes] = shift(edge_in[side].astype(f32), 64, 1).astype(bf16)
    enc_ed = dot(enc_wide[...], pick)
    pooled = jnp.where(inside, (enc_ed[:, 0:LANES] + enc_ed[:, LANES:]) * 0.5, 0.0)
    pooled_own[...] = pooled.astype(bf16)
    pair(0, pooled_own, pooled_other).start()
    second_step(0, 2)
    for m in (0, 1, 4, 5, 6):
        first(m, True).wait_recv()
    for n in range(4):
        second_start(1, n)
    swap(1, two)
    enc_rows[...] = dot(spread, enc_ed.astype(bf16)).reshape(RING, ROWS, 2 * LANES).astype(bf16)
    cot_ed = dot(cot_wide[...], pick).astype(bf16)
    cot_rows[...] = dot(spread, cot_ed).reshape(RING, ROWS, 2 * LANES).astype(bf16)
    pair(0, pooled_own, pooled_other).wait_recv()
    for other, ref in enumerate((pooled_own, pooled_other)):
        value = ref[...].astype(f32)
        for k in range(5):
            start = other * L1 + k * FINE_C
            x1[start : start + FINE_C] = shift(value, 2 - k, 1).astype(bf16)
        x1[other * L1 + 880 : (other + 1) * L1] = jnp.zeros((16, LANES), bf16)
    second_step(0, 3)
    for n in range(4):
        second_part(1, 1, n)
    second_swap(1, 1)
    second_step(0, 4)
    second_step(1, 2)

    for c in (0, 1):
        if c == 0:
            swap_done(0)

        @pl.loop(2 * c, 2 * c + 2)
        def _(q):
            swapped = dot(flat(w1_swap[q]), x1[L1 : 2 * L1])

            def use(mine):
                part = dot(mine[0], x1[0:L1]) + swapped
                p1_send[:, q] = part.reshape(RING, ROWS, LANES).astype(bf16)

            own_taps(0, [q], use)

        for d in order:
            scatter(0, c, p1_send, p1_recv, d).start()

    p1_recv[t] = p1_send[t]
    second_step(1, 3)
    for c in (0, 1):
        for d in order:
            scatter(0, c, p1_send, p1_recv, d).wait_recv()
    sides = [sum(p1_recv[2 * x + p].astype(f32) for x in range(4)) for p in (0, 1)]
    pre_c[...] = jnp.stack(sides, axis=1).reshape(COARSE_C, LANES)
    c_own[...] = jnp.where(inside, gelu_value(pre_c[...]), 0.0).astype(bf16)
    pair(1, c_own, c_other).start()
    slope_c[...] = gelu_slope(pre_c[...])
    pair(1, c_own, c_other).wait_recv()
    for other, ref in enumerate((c_own, c_other)):
        value = ref[...]
        wide = value.astype(f32)
        before, after = shift(wide, 1, 1).astype(bf16), shift(wide, -1, 1).astype(bf16)
        for start, even, odd in (
            (0, before, before),
            (192, value, value),
            (384, after, after),
            (640, before, value),
            (832, value, after),
        ):
            start += other * L2
            x2[start : start + COARSE_C, 0:LANES] = even
            x2[start : start + COARSE_C, LANES : 2 * LANES] = odd
        x2[other * L2 + 576 : other * L2 + 640] = jnp.zeros((64, 2 * LANES), bf16)
    fine_swap_done(0)
    conv_fine([(slot, i) for slot in range(3) for i in rows_near])
    fine_sums(0, begun)
    second_step(1, 4)
    fine_swap_done(1)
    conv_fine([(slot, far) for slot in range(4)] + [(3, i) for i in rows_near])
    fine_sums(1, begun)
    p2_recv[t] = p2_send[t]

    def fine_slot(slot):
        for p in (0, 1):
            pre = sum(p2_recv[2 * x + p, slot].astype(f32) for x in range(4))
            value, slope = gelu_both(pre)
            at = column(p, slot)
            merged_rows[at] = (enc_rows[at].astype(f32) + value).astype(bf16)
            grad = (cot_rows[at].astype(f32) * slope).astype(bf16).astype(f32)
            even = jnp.where(inside, grad[:, 0:LANES], 0.0)
            odd = jnp.where(inside, grad[:, LANES:], 0.0)
            g_send[p, slot, :, 0:LANES] = (even + odd).astype(bf16)
            g_send[p, slot, :, LANES : 2 * LANES] = (even + shift(odd, 1, 1)).astype(bf16)

    @pl.when(t != far)
    def _():
        for d in order:
            fine_copy(2, d, p2_send, p2_recv, t, early).wait_recv()
        pl.loop(0, 3)(fine_slot)
        for d in order:
            fine_copy(4, d, g_send, g_recv, lax.rem(lax.rem(t + d, GROUPS), 2), early).start()
        for d in order:
            fine_copy(3, d, p2_send, p2_recv, t, late).wait_recv()

    @pl.when(t == far)
    def _():
        for d in order:
            fine_copy(3, d, p2_send, p2_recv, t, whole).wait_recv()
        pl.loop(0, 3)(fine_slot)

    fine_slot(3)
    fine_grads(1, begun, False)
    g_recv[t] = g_send[core]
    for side in (0, 1):
        halo(side).wait_send()
    for d in range(1, RING):
        near(d).wait_send()
    for m in range(7):
        first(m).wait_send()
    for w in (0, 1):
        for side in (0, 1):
            for n in range(4):
                for hop in (1, 2, 3, 4):
                    if hop < 4 or side == last_side(n):
                        second(w, side, hop, n).wait_send()
        swap_sent(w)
    pair(0, pooled_own, pooled_other).wait_send()
    pair(1, c_own, c_other).wait_send()
    for c in (0, 1):
        for d in order:
            scatter(0, c, p1_send, p1_recv, d).wait_send()
    back = iota((2 * LANES, FINE), 1)
    unpick = jnp.where(
        iota((2 * LANES, FINE), 0) == lax.rem(back, 2) * LANES + lax.div(back, 2) + EDGE, 1.0, 0.0
    ).astype(bf16)
    kept = dot_first(spread, flat(merged_rows[...])).astype(bf16)
    out_ref[0] = dot(kept, unpick).astype(bf16)

    fine_grads(0, arrived, True)
    fine_grads(1, arrived, True)
    columns = [lax.div(column(core, slot), 2) for slot in range(4)]
    block = jnp.concatenate([flat(g_recv[:, slot]) for slot in range(4)], axis=0)

    def back_fine(other, use):
        use = jnp.concatenate(use, axis=0)
        y1[other] = dot_first(block[:, 0:LANES], use[:, 0:640])
        y2[other] = dot_first(block[:, LANES:], use[:, 640:1024])

    back_fine(1, [flat(w2_swap[n]) for n in columns])

    def coarse_part(other):
        total = shift(y1[other, :, 0:192] + y2[other, :, 0:192], -1, 0)
        total = total + y1[other, :, 192:384] + y2[other, :, 192:384]
        total = total + shift(y1[other, :, 384:576], 1, 0)
        return transposed(total, COARSE_C)

    gc_out[...] = coarse_part(1)
    pair(2, gc_out, gc_in).start()
    own_taps(1, columns, lambda use: back_fine(0, use))
    own = coarse_part(0)
    pair(2, gc_out, gc_in).wait_recv()
    grad_c = jnp.where(inside, (own + gc_in[...]) * slope_c[...], 0.0).reshape(4, 2, ROWS, LANES).astype(bf16)
    gc_send[0] = grad_c[:, 0]
    gc_send[1] = grad_c[:, 1]
    for c in (0, 1):
        for d in order:
            gather(6, c, gc_send, gc_recv, d).start()
    gc_recv[t] = gc_send[core]
    pair(2, gc_out, gc_in).wait_send()
    for last in (0, 1):
        fine_sums(last, left)
        fine_grads(last, left, False)
    coarse_row = iota((LANES, FINE), 0)
    widen = jnp.where(coarse_row == lax.div(iota((LANES, FINE), 1), 2) + EDGE, 1.0, 0.0).astype(bf16)
    for c in (0, 1):
        for d in order:
            gather(6, c, gc_send, gc_recv, d).wait_recv()

        coarse_block = jnp.concatenate([flat(gc_recv[:, 2 * c + n]) for n in (0, 1)], axis=0)
        pair_of = [2 * c, 2 * c + 1]

        def back_coarse(other, use, c=c, coarse_block=coarse_block):
            part = dot_first(coarse_block, jnp.concatenate(use, axis=0))
            if c == 0:
                y4[other] = part
            else:
                y4[other] += part

        back_coarse(1, [flat(w1_swap[n]) for n in pair_of])
        if c == 0:
            own_taps(0, pair_of, lambda use: back_coarse(0, use))

    def fine_part(other):
        total = None
        for k in range(5):
            term = shift(y4[other, :, k * FINE_C : (k + 1) * FINE_C], k - 2, 0)
            total = term if total is None else total + term
        return transposed(total, FINE_C)

    gp_out[...] = fine_part(1)
    pair(3, gp_out, gp_in).start()
    own_taps(0, pair_of, lambda use: back_coarse(0, use))
    own = fine_part(0)
    for c in (0, 1):
        for d in order:
            gather(6, c, gc_send, gc_recv, d).wait_send()
    pair(3, gp_out, gp_in).wait_recv()
    total = (own + gp_in[...]) * 0.5
    high = total.astype(bf16)
    low = (total - high.astype(f32)).astype(bf16)
    out_ref[1] = (cot_wide[:, 128 : 128 + FINE].astype(f32) + dot(high, widen) + dot(low, widen)).astype(bf16)

    pair(3, gp_out, gp_in).wait_send()


def shards(enc, w_down, w_up, cot):
    dma = pltpu.SemaphoreType.DMA
    vmem = pltpu.VMEM
    both = pl.pallas_call(
        kernel,
        out_shape=jax.ShapeDtypeStruct((2, FINE_C, FINE), bf16),
        in_specs=[pl.BlockSpec(memory_space=pltpu.HBM)] * 4,
        out_specs=pl.BlockSpec(memory_space=vmem),
        scratch_shapes=[
            vmem((5, OUT1, FINE_C), bf16),
            vmem((5, OUT2, COARSE_C), bf16),
            vmem((2, FINE_C, 128), bf16),
            vmem((2, FINE_C, 128), bf16),
            vmem((FINE_C, WIDE), bf16),
            vmem((FINE_C, WIDE), bf16),
            vmem((RING, 4, 2, ROWS, L1), bf16),
            vmem((4, 4, 2, ROWS, L1), bf16),
            vmem((RING, 4, 2, ROWS, L2), bf16),
            vmem((4, 4, 2, ROWS, L2), bf16),
            vmem((FINE_C, LANES), bf16),
            vmem((FINE_C, LANES), bf16),
            vmem((2 * L1, LANES), bf16),
            vmem((GROUPS, 4, ROWS, LANES), bf16),
            vmem((GROUPS, 4, ROWS, LANES), bf16),
            vmem((COARSE_C, LANES), f32),
            vmem((COARSE_C, LANES), f32),
            vmem((COARSE_C, LANES), bf16),
            vmem((COARSE_C, LANES), bf16),
            vmem((2 * L2, 2 * LANES), bf16),
            vmem((RING, ROWS, 2 * LANES), bf16),
            vmem((RING, ROWS, 2 * LANES), bf16),
            vmem((RING, ROWS, 2 * LANES), bf16),
            vmem((GROUPS, 4, ROWS, 2 * LANES), bf16),
            vmem((GROUPS, 4, ROWS, 2 * LANES), bf16),
            vmem((2, 4, ROWS, 2 * LANES), bf16),
            vmem((GROUPS, 4, ROWS, 2 * LANES), bf16),
            vmem((2, LANES, 640), f32),
            vmem((2, LANES, 384), f32),
            vmem((COARSE_C, LANES), f32),
            vmem((COARSE_C, LANES), f32),
            vmem((2, 4, ROWS, LANES), bf16),
            vmem((GROUPS, 4, ROWS, LANES), bf16),
            vmem((2, LANES, L1), f32),
            vmem((FINE_C, LANES), f32),
            vmem((FINE_C, LANES), f32),
            dma((4,)),
            dma((2,)),
            dma((2,)),
            dma((RING,)),
            dma((RING,)),
            dma((7,)),
            dma((7,)),
            dma((2, 2, 5, 4)),
            dma((2, 2, 5, 4)),
            dma((2, RING)),
            dma((2, RING)),
            dma((4,)),
            dma((4,)),
            dma((8, GROUPS)),
            dma((8, GROUPS)),
        ],
        compiler_params=pltpu.CompilerParams(
            collective_id=0, has_side_effects=True, vmem_limit_bytes=VMEM_LIMIT
        ),
    )(enc[0], cot[0], jnp.swapaxes(w_down, 1, 2), jnp.swapaxes(w_up, 1, 2))
    return both[0:1], both[1:2]


def solution(mesh):
    placed = P(None, "tp", "ctx")
    return jax.shard_map(
        shards,
        mesh=mesh,
        in_specs=(placed,) * 4,
        out_specs=(placed, placed),
        check_vma=False,
    )
```
